32 devices in a mesh: pair: 2 (over x), grow: 4 (over z), gcol: 4 (over y, core).
Axes of the slice: x: 2, y: 2, z: 4, core: 2. Of those that a mesh axis runs over, the one named last changes fastest.
Arguments:
- valence: bfloat16 [2, 64, 128, 16384], P(None, None, ('grow', 'gcol')), may hold values from -6 to 6
- conduction: bfloat16 [2, 2, 128, 16384], P(None, 'pair', ('grow', 'gcol')), may hold values from -6 to 6
- pair_bands: int32 [2, 32], P('pair'), may hold values from 0 to 63, as said below
- e_val: float32 [64], replicated, may hold values from -12 to -1
- e_cond: float32 [2], P('pair'), may hold values from 1 to 12
- g_index: int32 [3840], replicated, may hold values from 0 to 2097151, as said below
- slab_index: int32 [256], replicated, may hold values from 0 to 2097151, as said below
Outputs:
- chi_slab: float32 [2, 3840, 256], P(None, ('pair', 'grow'), 'gcol')
The draws below stay inside these ranges and needn't reach their ends.
Inputs may be any that keep to these rules, and one draw needn't show every extreme that they name: `pair_bands`: each row lists 32 different valence bands. All entries of g_index and slab_index name different grid points. Write G = ((p * 4 + g) * 4 + c) * 120 + j with j < 120; the grid point of row G has q2 within [c * 32, (c + 1) * 32) and q3 within [b w, (b + 1) w) with b = g * 4 + c and w = 8. `slab_index`: write H = ((c * 2 + p) * 4 + g) * 8 + j with j < 8; the grid point of column H lies in the same range of q2 and q3 as the rows of g_index with these g and c.
All inputs are finite; a program needn't handle non-finite values.
Results may differ from the reference program's by a relative error of at most 0.012.
Values may be sent and summed in bfloat16 or wider, within the bound.
A program may use at most 256 MiB of HBM per device.

```python
import math
import jax
import jax.numpy as jnp
from jax import lax

NGRID = 128
NVAL = 64
PV = 32
GQ = 120
GCQ = 8
NC = 2
PAIRS = 64
NG = 3840
GC = 256
N_PAIR = 2
N_GROW = 4
N_GCOL = 4


def grid_picks(key):
    blocks = N_GROW * N_GCOL
    planes = NGRID // blocks
    wide_two = NGRID // N_GCOL
    count = NGRID * wide_two * planes
    keys = jax.random.split(key, blocks)
    orders = jax.vmap(lambda one: jax.random.permutation(one, count))(keys)
    needed = N_PAIR * (GQ + GCQ)
    offsets = orders[:, :needed].astype(jnp.int32)
    block_ids = jnp.arange(blocks, dtype=jnp.int32)
    gcol_of = block_ids % N_GCOL
    first = offsets // (wide_two * planes)
    second = gcol_of[:, None] * wide_two + offsets // planes % wide_two
    third = block_ids[:, None] * planes + offsets % planes
    return ((first * NGRID + second) * NGRID + third).astype(jnp.int32)


def draw_g_index(key, part):
    picks = grid_picks(key)
    rows = picks[:, :N_PAIR * GQ].reshape(N_GROW, N_GCOL, N_PAIR, GQ)
    return jnp.transpose(rows, (2, 0, 1, 3)).reshape(-1).astype(jnp.int32)


def draw_slab_index(key, part):
    picks = grid_picks(key)
    cols = picks[:, N_PAIR * GQ:].reshape(N_GROW, N_GCOL, N_PAIR, GCQ)
    return jnp.transpose(cols, (1, 2, 0, 3)).reshape(-1).astype(jnp.int32)


def draw_pair_bands(key, part):
    key = jax.random.fold_in(key, 3)
    keys = jax.random.split(key, NC + 2)
    chosen = jax.vmap(lambda one: jax.random.permutation(one, NVAL)[:PV])(keys[:NC])
    middle = jax.random.permutation(keys[NC], NVAL - 2)[:PV - 2] + 1
    ends = jnp.array([0, NVAL - 1], dtype=jnp.int32)
    first_row = jax.random.permutation(keys[NC + 1], jnp.concatenate([ends, middle.astype(jnp.int32)]))
    chosen = chosen.astype(jnp.int32).at[0].set(first_row.astype(jnp.int32))
    return chosen.astype(jnp.int32)


def levels(stream_key, shape, shards, low, top_value):
    gain, own = 1.0, jax.random.fold_in(stream_key, 6)
    for position, parts in shards:
        draws = jnp.exp(jax.random.uniform(jax.random.fold_in(own, position), (parts,), jnp.float32, low / len(shards), top_value / len(shards)))
        gain = gain * jnp.repeat(draws, shape[position] // parts).reshape([-1 if axis == position else 1 for axis in range(len(shape))])
    return gain


def scatter_about(key, shape, width, bound, shards=(), kind=jnp.bfloat16):
    gain = levels(key, shape, shards, -0.22, 0.18) if shards else 1.0
    drawn = jax.random.normal(key, shape, jnp.float32) * width * gain
    return jnp.minimum(jnp.maximum(drawn, -bound), bound).astype(kind)


def setup_inputs(seed: int = 0) -> dict:
    key_list = jax.random.split(jax.random.key(seed), 8)
    return {
        "valence": scatter_about(key_list[0], (2, NVAL, NGRID, NGRID * NGRID), 1.0, 6.0, ((2, 16),)),
        "conduction": scatter_about(key_list[1], (2, NC, NGRID, NGRID * NGRID), 1.0, 6.0, ((1, 2), (2, 16))),
        "pair_bands": draw_pair_bands(jax.random.fold_in(key_list[7], 71), 0),
        "e_val": jnp.clip(jax.random.uniform(key_list[3], (NVAL,), jnp.float32, -12.0, -1.0), -12.0, -1.0),
        "e_cond": jnp.clip(1.0 + 11.0 * jax.random.uniform(key_list[4], (NC,), jnp.float32) ** levels(key_list[4], (NC,), ((0, 2),), -0.2, 0.2), 1.0, 12.0),
        "g_index": draw_g_index(jax.random.fold_in(key_list[7], 71), 0),
        "slab_index": draw_slab_index(jax.random.fold_in(key_list[7], 71), 0),
    }


def transform_table(count):
    freq = jnp.arange(count, dtype=jnp.int32)
    phase = freq[:, None] * freq[None, :] % count
    angle = phase.astype(jnp.float32) * (2.0 * math.pi / count)
    scale = 1.0 / math.sqrt(count)
    cosine = (jnp.cos(angle) * scale).astype(jnp.bfloat16)
    sine = (jnp.sin(angle) * scale).astype(jnp.bfloat16)
    upper = jnp.stack([cosine, sine], axis=1)
    lower = jnp.stack([-sine, cosine], axis=1)
    return jnp.stack([upper, lower]).astype(jnp.float32)

def reference(valence, conduction, pair_bands, e_val, e_cond, g_index, slab_index):
    table = transform_table(NGRID)
    val_grid = valence.reshape(2, NVAL, NGRID, NGRID, NGRID)
    cond_grid = conduction.reshape(2, NC, NGRID, NGRID, NGRID)

    def one_band(band):
        chosen = pair_bands[band]
        picked = jnp.take(val_grid, chosen, axis=1).astype(jnp.float32)
        cond_now = cond_grid[:, band].astype(jnp.float32)
        real_part = picked[0] * cond_now[0][None] + picked[1] * cond_now[1][None]
        imag_part = picked[0] * cond_now[1][None] - picked[1] * cond_now[0][None]
        density = jnp.stack([real_part, imag_part]).astype(jnp.bfloat16)
        density = jnp.moveaxis(density, 1, 4).astype(jnp.float32)
        third = jnp.einsum('okix,iabxp->oabkp', table, density).astype(jnp.bfloat16)
        second = jnp.einsum('okix,iaxbp->oakbp', table, third.astype(jnp.float32)).astype(jnp.bfloat16)
        first = jnp.einsum('okix,ixabp->okabp', table, second.astype(jnp.float32)).astype(jnp.bfloat16)
        flat = first.reshape(2, NGRID * NGRID * NGRID, PV)
        weight = 2.0 / ((jnp.take(e_val, chosen) - e_cond[band]) * math.sqrt(PAIRS))
        rows = (jnp.take(flat, g_index, axis=1).astype(jnp.float32) * weight).astype(jnp.bfloat16)
        cols = jnp.take(flat, slab_index, axis=1)
        return (rows, cols)
    rows, cols = lax.map(one_band, jnp.arange(NC, dtype=jnp.int32))
    rows = jnp.transpose(rows, (1, 2, 0, 3)).reshape(2, NG, PAIRS).astype(jnp.float32)
    cols = jnp.transpose(cols, (1, 2, 0, 3)).reshape(2, GC, PAIRS).astype(jnp.float32)
    real_out = jnp.dot(rows[0], cols[0].T, preferred_element_type=jnp.float32) + jnp.dot(rows[1], cols[1].T, preferred_element_type=jnp.float32)
    imag_out = jnp.dot(rows[1], cols[0].T, preferred_element_type=jnp.float32) - jnp.dot(rows[0], cols[1].T, preferred_element_type=jnp.float32)
    return jnp.stack([real_out, imag_out])
```

```python
import math

import jax
import jax.numpy as jnp
from jax import lax
from jax.experimental import pallas as pl
from jax.experimental.pallas import tpu as pltpu
from jax.sharding import PartitionSpec as P

NGRID = 128


def transform_table(count, positions):
    freq = jnp.arange(count, dtype=jnp.int32)
    phase = freq[:, None] * positions[None, :] % count
    angle = phase.astype(jnp.float32) * (2.0 * math.pi / count)
    scale = 1.0 / math.sqrt(count)
    cosine = (jnp.cos(angle) * scale).astype(jnp.bfloat16)
    sine = (jnp.sin(angle) * scale).astype(jnp.bfloat16)
    upper = jnp.stack([cosine, sine], axis=1)
    lower = jnp.stack([-sine, cosine], axis=1)
    return jnp.stack([upper, lower])


def on_device_general(valence, conduction, pair_bands, e_val, e_cond, g_index, slab_index):
    n_pair = lax.axis_size("pair")
    n_grow = lax.axis_size("grow")
    n_gcol = lax.axis_size("gcol")
    grow_at = lax.axis_index("grow")
    gcol_at = lax.axis_index("gcol")
    planes = valence.shape[2]
    bands_here, partners = pair_bands.shape
    pairs_here = bands_here * partners
    total_pairs = pairs_here * n_pair
    picked = jnp.take(valence, pair_bands.reshape(-1), axis=1).astype(jnp.float32)
    cond_rep = jnp.repeat(conduction, partners, axis=1).astype(jnp.float32)
    real_part = picked[0] * cond_rep[0] + picked[1] * cond_rep[1]
    imag_part = picked[0] * cond_rep[1] - picked[1] * cond_rep[0]
    density = jnp.stack([real_part, imag_part]).astype(jnp.bfloat16)
    density = jnp.transpose(density.reshape(2, pairs_here, planes, NGRID, NGRID), (0, 2, 3, 4, 1))
    natural = transform_table(NGRID, jnp.arange(NGRID, dtype=jnp.int32))
    third = jnp.einsum(
        "okix,iabxp->oabkp", natural, density, preferred_element_type=jnp.float32
    ).astype(jnp.bfloat16)
    second = jnp.einsum(
        "okix,iaxbp->oakbp", natural, third, preferred_element_type=jnp.float32
    ).astype(jnp.bfloat16)
    moved = lax.all_to_all(second, ("grow", "gcol"), split_axis=3, concat_axis=1, tiled=True)
    positions = jnp.arange(NGRID, dtype=jnp.int32)
    wide_two = NGRID
    base_three = (grow_at * n_gcol + gcol_at) * planes
    table_first = transform_table(NGRID, positions)
    elements = jnp.einsum(
        "okix,ixabp->okabp", table_first, moved, preferred_element_type=jnp.float32
    ).astype(jnp.bfloat16)
    flat = elements.reshape(2, -1, pairs_here)

    def local_offset(index):
        first_q = index // (NGRID * NGRID)
        second_q = index // NGRID % NGRID
        third_q = index % NGRID
        return (first_q * wide_two + second_q) * planes + third_q - base_three

    row_count = g_index.shape[0] // (n_pair * n_grow * n_gcol)
    row_ids = g_index.reshape(n_pair, n_grow, n_gcol, row_count)[:, grow_at, gcol_at]
    rows = jnp.take(flat, local_offset(row_ids).reshape(-1), axis=1).reshape(
        2, n_pair, row_count, pairs_here
    )
    gaps = jnp.take(e_val, pair_bands) - e_cond[:, None]
    weight = (2.0 / (gaps * math.sqrt(total_pairs))).reshape(-1)
    weighted = (rows.astype(jnp.float32) * weight).astype(jnp.bfloat16)
    col_count = slab_index.shape[0] // (n_pair * n_grow * n_gcol)
    col_ids = slab_index.reshape(n_gcol, n_pair, n_grow, col_count)[gcol_at, :, grow_at]
    cols = jnp.take(flat, local_offset(col_ids).reshape(-1), axis=1).reshape(
        2, n_pair, col_count, pairs_here
    )
    row_block = lax.all_to_all(weighted, "pair", split_axis=1, concat_axis=3, tiled=True).reshape(
        2, row_count, total_pairs
    )
    spread = lax.all_gather(
        cols.reshape(2, n_pair, 1, col_count, pairs_here), "grow", axis=2, tiled=True
    )
    slab = lax.all_gather(spread, "pair", axis=4, tiled=True).reshape(2, -1, total_pairs)
    conjugate = jnp.stack([jnp.stack([slab[0], slab[1]]), jnp.stack([-slab[1], slab[0]])])
    return jnp.einsum(
        "irk,oick->orc",
        lax.all_gather(row_block, "gcol", axis=1, tiled=True),
        conjugate,
        preferred_element_type=jnp.float32,
    )


CHUNK = 16
BLOCK_ROWS = 128


def partial_kernel(bands, val, cond, t3, a2, pick, phase, spread, pack, out, vbuf, stage, third, sems):
    pairs, planes = vbuf.shape[1], vbuf.shape[2]
    lanes = pairs * planes
    wide = CHUNK * NGRID
    chunks = NGRID // CHUNK
    for chunk in range(chunks):
        at = pl.ds(chunk * wide, wide)

        @pl.loop(0, pairs)
        def _(pair):
            pltpu.make_async_copy(
                val.at[:, bands[pair], :, at], vbuf.at[:, pair, :, at], sems.at[chunk]
            ).start()

    @pl.loop(0, chunks)
    def _(chunk):
        at = pl.ds(pl.multiple_of(chunk * wide, wide), wide)
        pltpu.make_async_copy(
            vbuf.at[:, :, :, at], vbuf.at[:, :, :, at], sems.at[chunk]
        ).wait()

        @pl.loop(0, CHUNK)
        def _(step):
            here = pl.ds(pl.multiple_of(chunk * wide + step * NGRID, NGRID), NGRID)
            c_re = cond[0, :, here].astype(jnp.float32)
            c_im = cond[1, :, here].astype(jnp.float32)
            reals, imags = [], []
            for pair in range(pairs):
                v_re = vbuf[0, pair, :, here].astype(jnp.float32)
                v_im = vbuf[1, pair, :, here].astype(jnp.float32)
                reals.append(v_re * c_re + v_im * c_im)
                imags.append(v_re * c_im - v_im * c_re)
            density = jnp.concatenate(
                [jnp.concatenate(reals, axis=0), jnp.concatenate(imags, axis=0)], axis=1
            ).astype(jnp.bfloat16)
            moved = lax.dot_general(
                t3[...], density, (((1,), (1,)), ((), ())), preferred_element_type=jnp.float32
            )
            for half in range(lanes // 128):
                stage[half, pl.ds(step, 2 * NGRID, stride=CHUNK), :] = moved[
                    :, half * 128 : (half + 1) * 128
                ]

        rows = pl.ds(pl.multiple_of(chunk * CHUNK, CHUNK), CHUNK)

        @pl.loop(0, 2 * NGRID // 8)
        def _(group):
            for inner in range(8):
                freq = group * 8 + inner
                for half in range(lanes // 128):
                    third[freq, rows, half * 128 : (half + 1) * 128] = stage[
                        half, pl.ds(pl.multiple_of(freq * CHUNK, CHUNK), CHUNK), :
                    ].astype(jnp.bfloat16)

    blocks = pick.shape[0]
    width = NGRID // blocks
    ranges = a2.shape[0]
    wide_two = NGRID // ranges

    @pl.loop(0, blocks)
    def _(block):
        table = a2[block % ranges]
        reals, imags = [], []
        for inner in range(width):
            freq = block * width + inner
            field = jnp.concatenate([third[freq], third[NGRID + freq]], axis=0)
            moved = jnp.dot(table, field, preferred_element_type=jnp.float32).astype(jnp.bfloat16)
            reals.append(moved[:wide_two])
            imags.append(moved[wide_two:])
        chosen = pick[block]
        re = jnp.dot(chosen, jnp.concatenate(reals, axis=0), preferred_element_type=jnp.float32)
        im = jnp.dot(chosen, jnp.concatenate(imags, axis=0), preferred_element_type=jnp.float32)
        both = jnp.dot(phase[block], spread[...], preferred_element_type=jnp.float32)
        cosine, sine = both[:, :lanes], both[:, lanes:]
        z_re = (cosine * re + sine * im).astype(jnp.bfloat16)
        z_im = (cosine * im - sine * re).astype(jnp.bfloat16)
        parts = []
        for part in range(z_re.shape[0] // BLOCK_ROWS):
            cut = slice(part * BLOCK_ROWS, (part + 1) * BLOCK_ROWS)
            parts += [z_re[cut], z_im[cut]]
        out[block] = jnp.dot(
            jnp.concatenate(parts, axis=1), pack[...], preferred_element_type=jnp.float32
        ).astype(out.dtype)


def partial_sums(bands, valence, cond, t3, a2, pick, phase, spread, pack):
    pairs, planes = bands.shape[0], valence.shape[2]
    lanes = pairs * planes
    blocks = pick.shape[0]
    vmem = pl.BlockSpec(memory_space=pltpu.VMEM)
    return pl.pallas_call(
        partial_kernel,
        out_shape=jax.ShapeDtypeStruct((blocks, BLOCK_ROWS, pack.shape[1]), jnp.bfloat16),
        in_specs=[pl.BlockSpec(memory_space=pltpu.SMEM), pl.BlockSpec(memory_space=pl.ANY)] + [vmem] * 7,
        out_specs=vmem,
        scratch_shapes=[
            pltpu.VMEM((2, pairs, planes, NGRID * NGRID), jnp.bfloat16),
            pltpu.VMEM((lanes // 128, 2 * NGRID * CHUNK, 128), jnp.float32),
            pltpu.VMEM((2 * NGRID, NGRID, lanes), jnp.bfloat16),
            pltpu.SemaphoreType.DMA((NGRID // CHUNK,)),
        ],
        compiler_params=pltpu.CompilerParams(vmem_limit_bytes=58 * 2**20),
        name="partial_sums",
    )(bands, valence, cond, t3, a2, pick, phase, spread, pack)


def prepare(valence, conduction, pair_bands, g_index, slab_index):
    n_pair = lax.axis_size("pair")
    n_grow = lax.axis_size("grow")
    n_gcol = lax.axis_size("gcol")
    blocks = n_grow * n_gcol
    me = lax.axis_index("grow") * n_gcol + lax.axis_index("gcol")
    planes = valence.shape[2]
    pairs = pair_bands.size
    lanes = pairs * planes
    rows = g_index.reshape(n_pair, n_grow, n_gcol, -1).transpose(1, 2, 0, 3)
    cols = slab_index.reshape(n_gcol, n_pair, n_grow, -1).transpose(2, 0, 1, 3)
    points = jnp.concatenate([rows, cols], axis=3).reshape(blocks, -1)
    wide_two = NGRID // n_gcol
    spot = (points % planes) * wide_two + points // NGRID % wide_two
    pick = (spot[:, :, None] == jnp.arange(planes * wide_two, dtype=jnp.int32)).astype(jnp.bfloat16)
    first = points // (NGRID * NGRID)
    where = me * planes + jnp.arange(planes, dtype=jnp.int32)
    angle = (first[:, :, None] * where % NGRID).astype(jnp.float32) * (2.0 * math.pi / NGRID)
    scale = 1.0 / math.sqrt(NGRID)
    phase = jnp.concatenate([jnp.cos(angle) * scale, jnp.sin(angle) * scale], axis=2).astype(jnp.bfloat16)
    lane = jnp.arange(2 * lanes, dtype=jnp.int32)
    kind = lane // lanes * planes + lane % planes
    spread = (jnp.arange(2 * planes, dtype=jnp.int32)[:, None] == kind).astype(jnp.bfloat16)
    source = jnp.arange(2 * n_pair * lanes, dtype=jnp.int32)
    target = source // lanes * pairs + source % lanes // planes
    pack = (target[:, None] == jnp.arange(2 * n_pair * pairs, dtype=jnp.int32)).astype(jnp.bfloat16)
    table = transform_table(NGRID, jnp.arange(NGRID, dtype=jnp.int32))
    t3 = table.reshape(2 * NGRID, 2 * NGRID)
    a2 = table.reshape(2, n_gcol, wide_two, 2 * NGRID).transpose(1, 0, 2, 3)
    a2 = a2.reshape(n_gcol, 2 * wide_two, 2 * NGRID)
    cond = conduction.reshape(2, planes, NGRID * NGRID)
    return pair_bands.reshape(-1), valence, cond, t3, a2, pick, phase, spread, pack


def on_device(valence, conduction, pair_bands, e_val, e_cond, g_index, slab_index):
    if valence.shape[2] != 8 or pair_bands.size != 32:
        return on_device_general(valence, conduction, pair_bands, e_val, e_cond, g_index, slab_index)
    n_pair = lax.axis_size("pair")
    n_grow = lax.axis_size("grow")
    n_gcol = lax.axis_size("gcol")
    pairs = pair_bands.size
    sums = partial_sums(*prepare(valence, conduction, pair_bands, g_index, slab_index))
    swapped = lax.all_to_all(sums, ("grow", "gcol"), split_axis=0, concat_axis=0, tiled=True)
    elements = jnp.sum(swapped.astype(jnp.float32), axis=0).astype(jnp.bfloat16)
    gaps = jnp.take(e_val, pair_bands) - e_cond[:, None]
    weight = (2.0 / (gaps * math.sqrt(pairs * n_pair))).reshape(-1)
    row_count = g_index.shape[0] // (n_pair * n_grow * n_gcol)
    weighted = (elements[:row_count].astype(jnp.float32) * jnp.tile(weight, 2 * n_pair)).astype(jnp.bfloat16)
    rows = lax.all_gather(weighted, ("pair", "gcol"), axis=0, tiled=False)
    rows = rows.reshape(n_pair, n_gcol, row_count, n_pair, 2, pairs)
    rows = lax.dynamic_index_in_dim(rows, lax.axis_index("pair"), axis=3, keepdims=False)
    cols = lax.all_gather(elements[row_count:], ("pair", "grow"), axis=0, tiled=False)
    cols = cols.reshape(n_pair, n_grow, -1, n_pair, 2, pairs)
    conjugate = jnp.stack([jnp.stack([cols[..., 0, :], cols[..., 1, :]]), jnp.stack([-cols[..., 1, :], cols[..., 0, :]])])
    result = jnp.einsum(
        "scjik,oisgnpk->ocjpgn", rows, conjugate, preferred_element_type=jnp.float32
    )
    return result.reshape(2, n_gcol * row_count, -1)


def solution(mesh):
    in_specs = (
        P(None, None, ("grow", "gcol"), None),
        P(None, "pair", ("grow", "gcol"), None),
        P("pair", None),
        P(),
        P("pair"),
        P(),
        P(),
    )
    out_specs = P(None, ("pair", "grow"), "gcol")
    return jax.shard_map(
        on_device, mesh=mesh, in_specs=in_specs, out_specs=out_specs, check_vma=False
    )
```

```python
import functools
import math

import jax
import jax.numpy as jnp
from jax import lax
from jax.experimental import pallas as pl
from jax.experimental.pallas import tpu as pltpu
from jax.sharding import PartitionSpec as P

NGRID = 128


def transform_table(count, positions):
    freq = jnp.arange(count, dtype=jnp.int32)
    phase = freq[:, None] * positions[None, :] % count
    angle = phase.astype(jnp.float32) * (2.0 * math.pi / count)
    scale = 1.0 / math.sqrt(count)
    cosine = (jnp.cos(angle) * scale).astype(jnp.bfloat16)
    sine = (jnp.sin(angle) * scale).astype(jnp.bfloat16)
    upper = jnp.stack([cosine, sine], axis=1)
    lower = jnp.stack([-sine, cosine], axis=1)
    return jnp.stack([upper, lower])


def on_device_general(valence, conduction, pair_bands, e_val, e_cond, g_index, slab_index):
    n_pair = lax.axis_size("pair")
    n_grow = lax.axis_size("grow")
    n_gcol = lax.axis_size("gcol")
    grow_at = lax.axis_index("grow")
    gcol_at = lax.axis_index("gcol")
    planes = valence.shape[2]
    bands_here, partners = pair_bands.shape
    pairs_here = bands_here * partners
    total_pairs = pairs_here * n_pair
    picked = jnp.take(valence, pair_bands.reshape(-1), axis=1).astype(jnp.float32)
    cond_rep = jnp.repeat(conduction, partners, axis=1).astype(jnp.float32)
    real_part = picked[0] * cond_rep[0] + picked[1] * cond_rep[1]
    imag_part = picked[0] * cond_rep[1] - picked[1] * cond_rep[0]
    density = jnp.stack([real_part, imag_part]).astype(jnp.bfloat16)
    density = jnp.transpose(density.reshape(2, pairs_here, planes, NGRID, NGRID), (0, 2, 3, 4, 1))
    natural = transform_table(NGRID, jnp.arange(NGRID, dtype=jnp.int32))
    third = jnp.einsum(
        "okix,iabxp->oabkp", natural, density, preferred_element_type=jnp.float32
    ).astype(jnp.bfloat16)
    second = jnp.einsum(
        "okix,iaxbp->oakbp", natural, third, preferred_element_type=jnp.float32
    ).astype(jnp.bfloat16)
    moved = lax.all_to_all(second, ("grow", "gcol"), split_axis=3, concat_axis=1, tiled=True)
    positions = jnp.arange(NGRID, dtype=jnp.int32)
    wide_two = NGRID
    base_three = (grow_at * n_gcol + gcol_at) * planes
    table_first = transform_table(NGRID, positions)
    elements = jnp.einsum(
        "okix,ixabp->okabp", table_first, moved, preferred_element_type=jnp.float32
    ).astype(jnp.bfloat16)
    flat = elements.reshape(2, -1, pairs_here)

    def local_offset(index):
        first_q = index // (NGRID * NGRID)
        second_q = index // NGRID % NGRID
        third_q = index % NGRID
        return (first_q * wide_two + second_q) * planes + third_q - base_three

    row_count = g_index.shape[0] // (n_pair * n_grow * n_gcol)
    row_ids = g_index.reshape(n_pair, n_grow, n_gcol, row_count)[:, grow_at, gcol_at]
    rows = jnp.take(flat, local_offset(row_ids).reshape(-1), axis=1).reshape(
        2, n_pair, row_count, pairs_here
    )
    gaps = jnp.take(e_val, pair_bands) - e_cond[:, None]
    weight = (2.0 / (gaps * math.sqrt(total_pairs))).reshape(-1)
    weighted = (rows.astype(jnp.float32) * weight).astype(jnp.bfloat16)
    col_count = slab_index.shape[0] // (n_pair * n_grow * n_gcol)
    col_ids = slab_index.reshape(n_gcol, n_pair, n_grow, col_count)[gcol_at, :, grow_at]
    cols = jnp.take(flat, local_offset(col_ids).reshape(-1), axis=1).reshape(
        2, n_pair, col_count, pairs_here
    )
    row_block = lax.all_to_all(weighted, "pair", split_axis=1, concat_axis=3, tiled=True).reshape(
        2, row_count, total_pairs
    )
    spread = lax.all_gather(
        cols.reshape(2, n_pair, 1, col_count, pairs_here), "grow", axis=2, tiled=True
    )
    slab = lax.all_gather(spread, "pair", axis=4, tiled=True).reshape(2, -1, total_pairs)
    conjugate = jnp.stack([jnp.stack([slab[0], slab[1]]), jnp.stack([-slab[1], slab[0]])])
    return jnp.einsum(
        "irk,oick->orc",
        lax.all_gather(row_block, "gcol", axis=1, tiled=True),
        conjugate,
        preferred_element_type=jnp.float32,
    )


CHUNK = 16
PITCH = 17
BLOCK_ROWS = 128
MESH = pl.DeviceIdType.MESH


def partial_kernel(bands, val, cond, t3, a2, pick, phase, spread, pack, out, vbuf, stage, third, sems):
    pairs, planes = vbuf.shape[1], vbuf.shape[2]
    lanes = pairs * planes
    wide = CHUNK * NGRID
    chunks = NGRID // CHUNK
    def fetch(chunk, pair):
        at = pl.ds(chunk * wide, wide)
        return pltpu.make_async_copy(
            val.at[:, bands[pair], :, at], vbuf.at[:, pair, :, at], sems.at[chunk]
        )

    @pl.loop(0, pairs)
    def _(pair):
        fetch(0, pair).start()

    for chunk in range(chunks):
        at = pl.ds(chunk * wide, wide)
        if chunk + 1 < chunks:

            @pl.loop(0, pairs, unroll=4)
            def _(pair):
                fetch(chunk + 1, pair).start()

        pltpu.make_async_copy(
            vbuf.at[:, :, :, at], vbuf.at[:, :, :, at], sems.at[chunk]
        ).wait()

        @pl.loop(0, CHUNK, unroll=4)
        def _(step):
            here = pl.ds(pl.multiple_of(chunk * wide + step * NGRID, NGRID), NGRID)
            c_re = cond[0, :, here].astype(jnp.float32)
            c_im = cond[1, :, here].astype(jnp.float32)
            reals, imags = [], []
            for pair in range(pairs):
                v_re = vbuf[0, pair, :, here].astype(jnp.float32)
                v_im = vbuf[1, pair, :, here].astype(jnp.float32)
                reals.append(v_re * c_re + v_im * c_im)
                imags.append(v_re * c_im - v_im * c_re)
            density = jnp.concatenate(
                [jnp.concatenate(reals, axis=0), jnp.concatenate(imags, axis=0)], axis=1
            ).astype(jnp.bfloat16)
            moved = lax.dot_general(
                t3[...], density, (((1,), (1,)), ((), ())), preferred_element_type=jnp.float32
            )
            for half in range(lanes // 128):
                stage[half, pl.ds(step, 2 * NGRID, stride=PITCH), :] = moved[
                    :, half * 128 : (half + 1) * 128
                ]

        rows = pl.ds(chunk * CHUNK, CHUNK)

        @pl.loop(0, 2 * NGRID // 8)
        def _(group):
            for inner in range(8):
                freq = group * 8 + inner
                start = pl.multiple_of(group * (8 * PITCH), 8) + inner * PITCH
                for half in range(lanes // 128):
                    third[freq, rows, half * 128 : (half + 1) * 128] = stage[
                        half, pl.ds(start, CHUNK), :
                    ].astype(jnp.bfloat16)

    blocks = pick.shape[0]
    width = NGRID // blocks
    ranges = a2.shape[0]
    wide_two = NGRID // ranges

    @pl.loop(0, blocks)
    def _(block):
        table = a2[block % ranges]
        reals, imags = [], []
        for inner in range(width):
            freq = block * width + inner
            field = jnp.concatenate([third[freq], third[NGRID + freq]], axis=0)
            moved = jnp.dot(table, field, preferred_element_type=jnp.float32).astype(jnp.bfloat16)
            reals.append(moved[:wide_two])
            imags.append(moved[wide_two:])
        chosen = pick[block]
        re = jnp.dot(chosen, jnp.concatenate(reals, axis=0), preferred_element_type=jnp.float32)
        im = jnp.dot(chosen, jnp.concatenate(imags, axis=0), preferred_element_type=jnp.float32)
        both = jnp.dot(phase[block], spread[...], preferred_element_type=jnp.float32)
        cosine, sine = both[:, :lanes], both[:, lanes:]
        z_re = (cosine * re + sine * im).astype(jnp.bfloat16)
        z_im = (cosine * im - sine * re).astype(jnp.bfloat16)
        half = BLOCK_ROWS // 2
        parts = []
        for low in range(0, BLOCK_ROWS, half):
            for z in (z_re, z_im):
                starts = range(low, z.shape[0], BLOCK_ROWS)
                parts.append(jnp.concatenate([z[at : at + half] for at in starts], axis=0))
        out[block] = jnp.dot(
            jnp.concatenate(parts, axis=1), pack[...], preferred_element_type=jnp.float32
        ).astype(out.dtype)


def partial_sums(bands, valence, cond, t3, a2, pick, phase, spread, pack):
    pairs, planes = bands.shape[0], valence.shape[2]
    lanes = pairs * planes
    blocks = pick.shape[0]
    vmem = pl.BlockSpec(memory_space=pltpu.VMEM)
    return pl.pallas_call(
        partial_kernel,
        out_shape=jax.ShapeDtypeStruct((blocks, BLOCK_ROWS, pack.shape[1]), jnp.bfloat16),
        in_specs=[pl.BlockSpec(memory_space=pltpu.SMEM), pl.BlockSpec(memory_space=pl.ANY)] + [vmem] * 7,
        out_specs=vmem,
        scratch_shapes=[
            pltpu.VMEM((2, pairs, planes, NGRID * NGRID), jnp.bfloat16),
            pltpu.VMEM((lanes // 128, 2 * NGRID * PITCH, 128), jnp.float32),
            pltpu.VMEM((2 * NGRID, NGRID, lanes), jnp.bfloat16),
            pltpu.SemaphoreType.DMA((NGRID // CHUNK,)),
        ],
        compiler_params=pltpu.CompilerParams(vmem_limit_bytes=58 * 2**20),
        name="partial_sums",
    )(bands, valence, cond, t3, a2, pick, phase, spread, pack)


def finish_kernel(
    sizes, row_count, sums, weight, out, inbox, row_out, row_in, col_out, col_in,
    sum_send, sum_recv, row_send, row_recv, col_send, col_recv,
):
    n_pair, n_grow, n_gcol = sizes
    blocks = n_grow * n_gcol
    pair_at = lax.axis_index("pair")
    grow_at = lax.axis_index("grow")
    gcol_at = lax.axis_index("gcol")
    me = grow_at * n_gcol + gcol_at
    half = BLOCK_ROWS // 2
    col_count = BLOCK_ROWS - row_count

    def place(pair, grow, gcol):
        return {"pair": pair, "grow": grow, "gcol": gcol}

    def arrival(src, dst, send, recv):
        at = place(lax.rem(pair_at + 1, n_pair), grow_at, gcol_at)
        return pltpu.make_async_remote_copy(
            src_ref=src, dst_ref=dst, send_sem=send, recv_sem=recv, device_id=at, device_id_type=MESH
        )

    def block_place(distance):
        other = lax.rem(me + distance, blocks)
        return other, place(pair_at, other // n_gcol, lax.rem(other, n_gcol))

    barrier = pltpu.get_barrier_semaphore()
    greeted = 0
    for distance in range(1, blocks):
        pl.semaphore_signal(barrier, inc=1, device_id=block_place(distance)[1], device_id_type=MESH)
        greeted += 1
    for far in range(1, n_pair):
        other = lax.rem(pair_at + far, n_pair)
        for step in range(n_gcol):
            at = place(other, grow_at, lax.rem(gcol_at + step, n_gcol))
            pl.semaphore_signal(barrier, inc=1, device_id=at, device_id_type=MESH)
            greeted += 1
        for step in range(1, n_grow):
            at = place(other, lax.rem(grow_at + step, n_grow), gcol_at)
            pl.semaphore_signal(barrier, inc=1, device_id=at, device_id_type=MESH)
            greeted += 1
    pl.semaphore_wait(barrier, greeted)

    sum_copies = []
    for distance in range(1, blocks):
        other, at = block_place(distance)
        copy = pltpu.make_async_remote_copy(
            src_ref=sums.at[other], dst_ref=inbox.at[distance],
            send_sem=sum_send.at[distance], recv_sem=sum_recv.at[distance],
            device_id=at, device_id_type=MESH,
        )
        copy.start()
        sum_copies.append(copy)
    total = sums[me].astype(jnp.float32)
    for distance, copy in enumerate(sum_copies, 1):
        copy.wait_recv()
        total = total + inbox[distance].astype(jnp.float32)
    elements = total.astype(jnp.bfloat16).astype(jnp.float32)
    weighted = (elements * weight[...]).astype(jnp.bfloat16)
    cols = [elements[(one + 1) * half - col_count : (one + 1) * half] for one in range(n_pair)]
    cols = jnp.concatenate(cols, axis=0).astype(jnp.bfloat16)
    col_out[...] = cols
    for one in range(n_pair):
        row_out[one] = weighted[one * half : (one + 1) * half]
    row_slot = pair_at * n_gcol + gcol_at
    col_slot = pair_at * n_grow + grow_at
    row_copies, col_copies = [], []
    for far in range(n_pair):
        other = lax.rem(pair_at + far, n_pair)
        behind = lax.rem(pair_at + n_pair - far, n_pair)
        for step in range(n_grow):
            if far or step:
                number = far * n_grow + step
                copy = pltpu.make_async_remote_copy(
                    src_ref=col_out, dst_ref=col_in.at[col_slot],
                    send_sem=col_send.at[number], recv_sem=col_recv.at[col_slot],
                    device_id=place(other, lax.rem(grow_at + step, n_grow), gcol_at),
                    device_id_type=MESH,
                )
                copy.start()
                source = behind * n_grow + lax.rem(grow_at + n_grow - step, n_grow)
                col_copies.append((copy, source))
        for step in range(n_gcol):
            if far or step:
                number = far * n_gcol + step
                copy = pltpu.make_async_remote_copy(
                    src_ref=row_out.at[other], dst_ref=row_in.at[row_slot],
                    send_sem=row_send.at[number], recv_sem=row_recv.at[row_slot],
                    device_id=place(other, grow_at, lax.rem(gcol_at + step, n_gcol)),
                    device_id_type=MESH,
                )
                copy.start()
                source = behind * n_gcol + lax.rem(gcol_at + n_gcol - step, n_gcol)
                row_copies.append((copy, source))
    col_in[col_slot] = cols
    row_in[row_slot] = row_out[pair_at]
    for _, source in col_copies:
        arrival(col_out, col_in.at[source], col_send.at[0], col_recv.at[source]).wait_recv()
    lane = lax.broadcasted_iota(jnp.int32, (out.shape[2], 4 * (weight.shape[1] // 4)), 1)
    pairs = weight.shape[1] // 4
    tables = {}
    for one in range(n_pair):
        pieces = []
        for target in range(n_pair):
            for grow in range(n_grow):
                piece = col_in[one * n_grow + grow].astype(jnp.float32)
                pieces.append(piece[target * col_count : (target + 1) * col_count])
        straight = jnp.where(lane >= 2 * pairs, jnp.concatenate(pieces, axis=0), 0.0)
        crossed = jnp.where(
            lane >= 3 * pairs,
            pltpu.roll(straight, pairs, 1),
            jnp.where(lane >= 2 * pairs, -pltpu.roll(straight, 3 * pairs, 1), 0.0),
        )
        for part, table in enumerate((straight, crossed)):
            tables[one, 1, part] = table.astype(jnp.bfloat16)
            tables[one, 0, part] = pltpu.roll(table, 2 * pairs, 1).astype(jnp.bfloat16)
    for _, source in row_copies:
        arrival(row_out.at[0], row_in.at[source], row_send.at[0], row_recv.at[source]).wait_recv()
    rows = [
        jnp.concatenate([row_in[one * n_gcol + gcol] for gcol in range(n_gcol)], axis=0)
        for one in range(n_pair)
    ]
    rows = jnp.concatenate(rows, axis=1)
    for low in range(2):
        for part in range(2):
            table = jnp.concatenate([tables[one, low, part] for one in range(n_pair)], axis=1)
            made = lax.dot_general(
                rows, table, (((1,), (1,)), ((), ())), preferred_element_type=jnp.float32
            )
            count = min(half, row_count - low * half)
            for gcol in range(n_gcol):
                start = gcol * row_count + low * half
                out[part, start : start + count, :] = made[gcol * half : gcol * half + count]
    for copy in sum_copies:
        copy.wait_send()
    for copy, _ in col_copies + row_copies:
        copy.wait_send()


def finish(sums, weight, sizes, row_count):
    n_pair, n_grow, n_gcol = sizes
    blocks, _, width = sums.shape
    half = BLOCK_ROWS // 2
    col_count = BLOCK_ROWS - row_count
    vmem = pl.BlockSpec(memory_space=pltpu.VMEM)
    sem = pltpu.SemaphoreType.DMA
    out_shape = (2, n_gcol * row_count, n_pair * n_grow * col_count)
    return pl.pallas_call(
        functools.partial(finish_kernel, sizes, row_count),
        out_shape=jax.ShapeDtypeStruct(out_shape, jnp.float32),
        in_specs=[vmem, vmem],
        out_specs=vmem,
        scratch_shapes=[
            pltpu.VMEM((blocks, BLOCK_ROWS, width), jnp.bfloat16),
            pltpu.VMEM((n_pair, half, width), jnp.bfloat16),
            pltpu.VMEM((n_pair * n_gcol, half, width), jnp.bfloat16),
            pltpu.VMEM((n_pair * col_count, width), jnp.bfloat16),
            pltpu.VMEM((n_pair * n_grow, n_pair * col_count, width), jnp.bfloat16),
            sem((blocks,)), sem((blocks,)),
            sem((n_pair * n_gcol,)), sem((n_pair * n_gcol,)),
            sem((n_pair * n_grow,)), sem((n_pair * n_grow,)),
        ],
        compiler_params=pltpu.CompilerParams(
            collective_id=0, has_side_effects=True, vmem_limit_bytes=16 * 2**20
        ),
        name="finish",
    )(sums, weight)


def prepare(valence, conduction, pair_bands, g_index, slab_index):
    n_pair = lax.axis_size("pair")
    n_grow = lax.axis_size("grow")
    n_gcol = lax.axis_size("gcol")
    blocks = n_grow * n_gcol
    me = lax.axis_index("grow") * n_gcol + lax.axis_index("gcol")
    planes = valence.shape[2]
    pairs = pair_bands.size
    lanes = pairs * planes
    rows = g_index.reshape(n_pair, n_grow, n_gcol, -1).transpose(1, 2, 0, 3)
    cols = slab_index.reshape(n_gcol, n_pair, n_grow, -1).transpose(2, 0, 1, 3)
    points = jnp.concatenate([rows, cols], axis=3).reshape(blocks, -1)
    wide_two = NGRID // n_gcol
    spot = (points % planes) * wide_two + points // NGRID % wide_two
    pick = (spot[:, :, None] == jnp.arange(planes * wide_two, dtype=jnp.int32)).astype(jnp.bfloat16)
    first = points // (NGRID * NGRID)
    where = me * planes + jnp.arange(planes, dtype=jnp.int32)
    angle = (first[:, :, None] * where % NGRID).astype(jnp.float32) * (2.0 * math.pi / NGRID)
    scale = 1.0 / math.sqrt(NGRID)
    phase = jnp.concatenate([jnp.cos(angle) * scale, jnp.sin(angle) * scale], axis=2).astype(jnp.bfloat16)
    lane = jnp.arange(2 * lanes, dtype=jnp.int32)
    kind = lane // lanes * planes + lane % planes
    spread = (jnp.arange(2 * planes, dtype=jnp.int32)[:, None] == kind).astype(jnp.bfloat16)
    source = jnp.arange(4 * lanes, dtype=jnp.int32)
    target = source // lanes * pairs + source % lanes // planes
    pack = (target[:, None] == jnp.arange(4 * pairs, dtype=jnp.int32)).astype(jnp.bfloat16)
    table = transform_table(NGRID, jnp.arange(NGRID, dtype=jnp.int32))
    t3 = table.reshape(2 * NGRID, 2 * NGRID)
    a2 = table.reshape(2, n_gcol, wide_two, 2 * NGRID).transpose(1, 0, 2, 3)
    a2 = a2.reshape(n_gcol, 2 * wide_two, 2 * NGRID)
    cond = conduction.reshape(2, planes, NGRID * NGRID)
    return pair_bands.reshape(-1), valence, cond, t3, a2, pick, phase, spread, pack


def on_device(valence, conduction, pair_bands, e_val, e_cond, g_index, slab_index):
    if valence.shape[2] != 8 or pair_bands.size != 32:
        return on_device_general(valence, conduction, pair_bands, e_val, e_cond, g_index, slab_index)
    n_pair = lax.axis_size("pair")
    n_grow = lax.axis_size("grow")
    n_gcol = lax.axis_size("gcol")
    pairs = pair_bands.size
    sums = partial_sums(*prepare(valence, conduction, pair_bands, g_index, slab_index))
    gaps = jnp.take(e_val, pair_bands) - e_cond[:, None]
    weight = (2.0 / (gaps * math.sqrt(pairs * n_pair))).reshape(-1)
    row_count = g_index.shape[0] // (n_pair * n_grow * n_gcol)
    return finish(sums, jnp.tile(weight, 4)[None], (n_pair, n_grow, n_gcol), row_count)


def solution(mesh):
    in_specs = (
        P(None, None, ("grow", "gcol"), None),
        P(None, "pair", ("grow", "gcol"), None),
        P("pair", None),
        P(),
        P("pair"),
        P(),
        P(),
    )
    out_specs = P(None, ("pair", "grow"), "gcol")
    return jax.shard_map(
        on_device, mesh=mesh, in_specs=in_specs, out_specs=out_specs, check_vma=False
    )
```

```python
import functools
import math

import jax
import jax.numpy as jnp
import numpy as np
from jax import lax
from jax.experimental import pallas as pl
from jax.experimental.pallas import tpu as pltpu
from jax.sharding import PartitionSpec as P

NGRID = 128


def transform_table(count, positions):
    freq = jnp.arange(count, dtype=jnp.int32)
    phase = freq[:, None] * positions[None, :] % count
    angle = phase.astype(jnp.float32) * (2.0 * math.pi / count)
    scale = 1.0 / math.sqrt(count)
    cosine = (jnp.cos(angle) * scale).astype(jnp.bfloat16)
    sine = (jnp.sin(angle) * scale).astype(jnp.bfloat16)
    upper = jnp.stack([cosine, sine], axis=1)
    lower = jnp.stack([-sine, cosine], axis=1)
    return jnp.stack([upper, lower])


def on_device_general(valence, conduction, pair_bands, e_val, e_cond, g_index, slab_index):
    n_pair = lax.axis_size("pair")
    n_grow = lax.axis_size("grow")
    n_gcol = lax.axis_size("gcol")
    grow_at = lax.axis_index("grow")
    gcol_at = lax.axis_index("gcol")
    planes = valence.shape[2]
    bands_here, partners = pair_bands.shape
    pairs_here = bands_here * partners
    total_pairs = pairs_here * n_pair
    picked = jnp.take(valence, pair_bands.reshape(-1), axis=1).astype(jnp.float32)
    cond_rep = jnp.repeat(conduction, partners, axis=1).astype(jnp.float32)
    real_part = picked[0] * cond_rep[0] + picked[1] * cond_rep[1]
    imag_part = picked[0] * cond_rep[1] - picked[1] * cond_rep[0]
    density = jnp.stack([real_part, imag_part]).astype(jnp.bfloat16)
    density = jnp.transpose(density.reshape(2, pairs_here, planes, NGRID, NGRID), (0, 2, 3, 4, 1))
    natural = transform_table(NGRID, jnp.arange(NGRID, dtype=jnp.int32))
    third = jnp.einsum(
        "okix,iabxp->oabkp", natural, density, preferred_element_type=jnp.float32
    ).astype(jnp.bfloat16)
    second = jnp.einsum(
        "okix,iaxbp->oakbp", natural, third, preferred_element_type=jnp.float32
    ).astype(jnp.bfloat16)
    moved = lax.all_to_all(second, ("grow", "gcol"), split_axis=3, concat_axis=1, tiled=True)
    positions = jnp.arange(NGRID, dtype=jnp.int32)
    wide_two = NGRID
    base_three = (grow_at * n_gcol + gcol_at) * planes
    table_first = transform_table(NGRID, positions)
    elements = jnp.einsum(
        "okix,ixabp->okabp", table_first, moved, preferred_element_type=jnp.float32
    ).astype(jnp.bfloat16)
    flat = elements.reshape(2, -1, pairs_here)

    def local_offset(index):
        first_q = index // (NGRID * NGRID)
        second_q = index // NGRID % NGRID
        third_q = index % NGRID
        return (first_q * wide_two + second_q) * planes + third_q - base_three

    row_count = g_index.shape[0] // (n_pair * n_grow * n_gcol)
    row_ids = g_index.reshape(n_pair, n_grow, n_gcol, row_count)[:, grow_at, gcol_at]
    rows = jnp.take(flat, local_offset(row_ids).reshape(-1), axis=1).reshape(
        2, n_pair, row_count, pairs_here
    )
    gaps = jnp.take(e_val, pair_bands) - e_cond[:, None]
    weight = (2.0 / (gaps * math.sqrt(total_pairs))).reshape(-1)
    weighted = (rows.astype(jnp.float32) * weight).astype(jnp.bfloat16)
    col_count = slab_index.shape[0] // (n_pair * n_grow * n_gcol)
    col_ids = slab_index.reshape(n_gcol, n_pair, n_grow, col_count)[gcol_at, :, grow_at]
    cols = jnp.take(flat, local_offset(col_ids).reshape(-1), axis=1).reshape(
        2, n_pair, col_count, pairs_here
    )
    row_block = lax.all_to_all(weighted, "pair", split_axis=1, concat_axis=3, tiled=True).reshape(
        2, row_count, total_pairs
    )
    spread = lax.all_gather(
        cols.reshape(2, n_pair, 1, col_count, pairs_here), "grow", axis=2, tiled=True
    )
    slab = lax.all_gather(spread, "pair", axis=4, tiled=True).reshape(2, -1, total_pairs)
    conjugate = jnp.stack([jnp.stack([slab[0], slab[1]]), jnp.stack([-slab[1], slab[0]])])
    return jnp.einsum(
        "irk,oick->orc",
        lax.all_gather(row_block, "gcol", axis=1, tiled=True),
        conjugate,
        preferred_element_type=jnp.float32,
    )


CHUNK = 16
PITCH = 17
SLOTS = 3
BLOCK_ROWS = 128
MESH = pl.DeviceIdType.MESH


def slab_kernel(
    sizes, row_count, bands, e_val, e_cond, val, cond, points, t3, out,
    slot_a, slot_b, slot_c, stage, third, pack, spread, sums, inbox, row_out, row_in, col_out, col_in,
    sems, sum_send, sum_recv, row_send, row_recv, col_send, col_recv,
):
    n_pair, n_grow, n_gcol = sizes
    blocks = n_grow * n_gcol
    pair_at = lax.axis_index("pair")
    grow_at = lax.axis_index("grow")
    gcol_at = lax.axis_index("gcol")
    me = grow_at * n_gcol + gcol_at
    half = BLOCK_ROWS // 2
    col_count = BLOCK_ROWS - row_count
    pairs = bands.shape[0]
    held = (slot_a, slot_b, slot_c)
    slots = len(held)
    planes, wide = slot_a.shape[2], slot_a.shape[3]
    lanes = pairs * planes
    chunks = NGRID // CHUNK

    def place(pair, grow, gcol):
        return {"pair": pair, "grow": grow, "gcol": gcol}

    def arrival(src, dst, send, recv):
        at = place(lax.rem(pair_at + 1, n_pair), grow_at, gcol_at)
        return pltpu.make_async_remote_copy(
            src_ref=src, dst_ref=dst, send_sem=send, recv_sem=recv, device_id=at, device_id_type=MESH
        )

    def block_place(distance):
        other = lax.rem(me + distance, blocks)
        return other, place(pair_at, other // n_gcol, lax.rem(other, n_gcol))

    def fetch(chunk):
        return pltpu.make_async_copy(
            val.at[:, :, :, pl.ds(chunk * wide, wide)], held[chunk % slots], sems.at[chunk % slots]
        )

    for chunk in range(slots - 1):
        fetch(chunk).start()

    barrier = pltpu.get_barrier_semaphore()
    greeted = 0
    for distance in range(1, blocks):
        pl.semaphore_signal(barrier, inc=1, device_id=block_place(distance)[1], device_id_type=MESH)
        greeted += 1
    for far in range(1, n_pair):
        other = lax.rem(pair_at + far, n_pair)
        for step in range(n_gcol):
            at = place(other, grow_at, lax.rem(gcol_at + step, n_gcol))
            pl.semaphore_signal(barrier, inc=1, device_id=at, device_id_type=MESH)
            greeted += 1
        for step in range(1, n_grow):
            at = place(other, lax.rem(grow_at + step, n_grow), gcol_at)
            pl.semaphore_signal(barrier, inc=1, device_id=at, device_id_type=MESH)
            greeted += 1

    source = lax.broadcasted_iota(jnp.int32, pack.shape, 0)
    target = source // lanes * pairs + source % lanes // planes
    pack[...] = jnp.where(
        target == lax.broadcasted_iota(jnp.int32, pack.shape, 1), 1.0, 0.0
    ).astype(jnp.bfloat16)
    plane = lax.broadcasted_iota(jnp.int32, (NGRID, lanes), 1) % planes + me * planes
    expand = jnp.where(
        lax.broadcasted_iota(jnp.int32, (NGRID, lanes), 0) == plane, 1.0, 0.0
    ).astype(jnp.bfloat16)
    for part in range(2):
        spread[:, part * lanes : (part + 1) * lanes] = jnp.dot(
            t3[:NGRID, part * NGRID : (part + 1) * NGRID], expand, preferred_element_type=jnp.float32
        ).astype(jnp.bfloat16)
    spot_of = lax.broadcasted_iota(jnp.int32, (1, 4 * pairs), 1) % pairs
    energy = jnp.zeros((1, 4 * pairs), jnp.float32)
    for pair in range(pairs):
        energy = jnp.where(spot_of == pair, e_val[bands[pair]], energy)
    weight = 2.0 / ((energy - e_cond[0]) * math.sqrt(pairs * n_pair))

    for chunk in range(chunks):
        slot = held[chunk % slots]
        fetch(chunk).wait()
        if chunk + slots - 1 < chunks:
            fetch(chunk + slots - 1).start()

        @pl.loop(0, CHUNK, unroll=4)
        def _(step):
            there = pl.ds(pl.multiple_of(chunk * wide + step * NGRID, NGRID), NGRID)
            here = pl.ds(pl.multiple_of(step * NGRID, NGRID), NGRID)
            c_re = cond[0, 0, :, there].astype(jnp.float32)
            c_im = cond[1, 0, :, there].astype(jnp.float32)
            reals, imags = [], []
            for pair in range(pairs):
                v_re = slot[0, bands[pair], :, here].astype(jnp.float32)
                v_im = slot[1, bands[pair], :, here].astype(jnp.float32)
                reals.append(v_re * c_re + v_im * c_im)
                imags.append(v_re * c_im - v_im * c_re)
            density = jnp.concatenate(
                [jnp.concatenate(reals, axis=0), jnp.concatenate(imags, axis=0)], axis=1
            ).astype(jnp.bfloat16)
            moved = lax.dot_general(
                t3[...], density, (((1,), (1,)), ((), ())), preferred_element_type=jnp.float32
            )
            for part in range(lanes // 128):
                stage[part, pl.ds(step, 2 * NGRID, stride=PITCH), :] = moved[
                    :, part * 128 : (part + 1) * 128
                ]

        rows = pl.ds(chunk * CHUNK, CHUNK)

        @pl.loop(0, 2 * NGRID // 8)
        def _(group):
            for inner in range(8):
                freq = group * 8 + inner
                start = pl.multiple_of(group * (8 * PITCH), 8) + inner * PITCH
                for part in range(lanes // 128):
                    third[freq, rows, part * 128 : (part + 1) * 128] = stage[
                        part, pl.ds(start, CHUNK), :
                    ].astype(jnp.bfloat16)

    width = NGRID // blocks
    wide_two = NGRID // n_gcol
    count = points.shape[1]

    def partial_sums(block):
        first_row = pl.multiple_of(lax.rem(block, n_gcol) * wide_two, wide_two)
        table = jnp.concatenate(
            [t3[pl.ds(first_row, wide_two), :], t3[pl.ds(first_row + NGRID, wide_two), :]], axis=0
        )
        reals, imags = [], []
        for inner in range(width):
            freq = block * width + inner
            field = jnp.concatenate([third[freq], third[NGRID + freq]], axis=0)
            moved = jnp.dot(table, field, preferred_element_type=jnp.float32).astype(jnp.bfloat16)
            reals.append(moved[:wide_two])
            imags.append(moved[wide_two:])
        listed = points[pl.ds(block, 1), :]
        spot = (listed & (width - 1)) * wide_two + ((listed >> 7) & (wide_two - 1))
        chosen = jnp.where(
            lax.broadcasted_iota(jnp.int32, (width * wide_two, count), 0) == spot, 1.0, 0.0
        ).astype(jnp.bfloat16)
        wave = jnp.where(
            lax.broadcasted_iota(jnp.int32, (NGRID, count), 0) == (listed >> 14), 1.0, 0.0
        ).astype(jnp.bfloat16)

        def choose(mask, field):
            return lax.dot_general(
                mask, field, (((0,), (0,)), ((), ())), preferred_element_type=jnp.float32
            )

        re = choose(chosen, jnp.concatenate(reals, axis=0))
        im = choose(chosen, jnp.concatenate(imags, axis=0))
        both = choose(wave, spread[...])
        cosine, sine = both[:, :lanes], both[:, lanes:]
        z_re = (cosine * re + sine * im).astype(jnp.bfloat16)
        z_im = (cosine * im - sine * re).astype(jnp.bfloat16)
        parts = []
        for low in range(0, BLOCK_ROWS, half):
            for z in (z_re, z_im):
                starts = range(low, count, BLOCK_ROWS)
                parts.append(jnp.concatenate([z[at : at + half] for at in starts], axis=0))
        return jnp.dot(
            jnp.concatenate(parts, axis=1), pack[...], preferred_element_type=jnp.float32
        )

    def sum_copy(distance):
        other, at = block_place(distance)
        return pltpu.make_async_remote_copy(
            src_ref=sums.at[distance], dst_ref=inbox.at[distance],
            send_sem=sum_send.at[distance], recv_sem=sum_recv.at[distance],
            device_id=at, device_id_type=MESH,
        )

    pl.semaphore_wait(barrier, greeted)

    @pl.loop(1, blocks, unroll=3)
    def _(distance):
        sums[distance] = partial_sums(lax.rem(me + distance, blocks)).astype(jnp.bfloat16)
        sum_copy(distance).start()

    total = partial_sums(me)
    for distance in range(1, blocks):
        sum_copy(distance).wait_recv()
        total = total + inbox[distance].astype(jnp.float32)
    elements = total.astype(jnp.bfloat16).astype(jnp.float32)
    weighted = (elements * weight).astype(jnp.bfloat16)
    cols = [elements[(one + 1) * half - col_count : (one + 1) * half] for one in range(n_pair)]
    cols = jnp.concatenate(cols, axis=0).astype(jnp.bfloat16)
    col_out[...] = cols
    for one in range(n_pair):
        row_out[one] = weighted[one * half : (one + 1) * half]
    row_slot = pair_at * n_gcol + gcol_at
    col_slot = pair_at * n_grow + grow_at
    row_copies, col_copies = [], []
    for far in range(n_pair):
        other = lax.rem(pair_at + far, n_pair)
        behind = lax.rem(pair_at + n_pair - far, n_pair)
        for step in range(n_grow):
            if far or step:
                number = far * n_grow + step
                copy = pltpu.make_async_remote_copy(
                    src_ref=col_out, dst_ref=col_in.at[col_slot],
                    send_sem=col_send.at[number], recv_sem=col_recv.at[col_slot],
                    device_id=place(other, lax.rem(grow_at + step, n_grow), gcol_at),
                    device_id_type=MESH,
                )
                copy.start()
                source = behind * n_grow + lax.rem(grow_at + n_grow - step, n_grow)
                col_copies.append((copy, source))
        for step in range(n_gcol):
            if far or step:
                number = far * n_gcol + step
                copy = pltpu.make_async_remote_copy(
                    src_ref=row_out.at[other], dst_ref=row_in.at[row_slot],
                    send_sem=row_send.at[number], recv_sem=row_recv.at[row_slot],
                    device_id=place(other, grow_at, lax.rem(gcol_at + step, n_gcol)),
                    device_id_type=MESH,
                )
                copy.start()
                source = behind * n_gcol + lax.rem(gcol_at + n_gcol - step, n_gcol)
                row_copies.append((copy, source))
    col_in[col_slot] = cols
    row_in[row_slot] = row_out[pair_at]
    for _, source in col_copies:
        arrival(col_out, col_in.at[source], col_send.at[0], col_recv.at[source]).wait_recv()
    lane = lax.broadcasted_iota(jnp.int32, (out.shape[2], 4 * pairs), 1)
    tables = {}
    for one in range(n_pair):
        pieces = []
        for target in range(n_pair):
            for grow in range(n_grow):
                piece = col_in[one * n_grow + grow].astype(jnp.float32)
                pieces.append(piece[target * col_count : (target + 1) * col_count])
        straight = jnp.where(lane >= 2 * pairs, jnp.concatenate(pieces, axis=0), 0.0)
        crossed = jnp.where(
            lane >= 3 * pairs,
            pltpu.roll(straight, pairs, 1),
            jnp.where(lane >= 2 * pairs, -pltpu.roll(straight, 3 * pairs, 1), 0.0),
        )
        for part, table in enumerate((straight, crossed)):
            tables[one, 1, part] = table.astype(jnp.bfloat16)
            tables[one, 0, part] = pltpu.roll(table, 2 * pairs, 1).astype(jnp.bfloat16)
    for _, source in row_copies:
        arrival(row_out.at[0], row_in.at[source], row_send.at[0], row_recv.at[source]).wait_recv()
    rows = [
        jnp.concatenate([row_in[one * n_gcol + gcol] for gcol in range(n_gcol)], axis=0)
        for one in range(n_pair)
    ]
    rows = jnp.concatenate(rows, axis=1)
    for low in range(2):
        for part in range(2):
            table = jnp.concatenate([tables[one, low, part] for one in range(n_pair)], axis=1)
            made = lax.dot_general(
                rows, table, (((1,), (1,)), ((), ())), preferred_element_type=jnp.float32
            )
            kept = min(half, row_count - low * half)
            for gcol in range(n_gcol):
                start = gcol * row_count + low * half
                out[part, start : start + kept, :] = made[gcol * half : gcol * half + kept]
    for distance in range(1, blocks):
        sum_copy(distance).wait_send()
    for copy, _ in col_copies + row_copies:
        copy.wait_send()


def fixed_table():
    freq = np.arange(NGRID, dtype=np.int32)
    angle = (freq[:, None] * freq[None, :] % NGRID).astype(np.float32) * np.float32(2.0 * math.pi / NGRID)
    scale = np.float32(1.0 / math.sqrt(NGRID))
    cosine = np.cos(angle) * scale
    sine = np.sin(angle) * scale
    return np.block([[cosine, sine], [-sine, cosine]]).astype(jnp.bfloat16)


def on_device(valence, conduction, pair_bands, e_val, e_cond, g_index, slab_index):
    n_pair = lax.axis_size("pair")
    n_grow = lax.axis_size("grow")
    n_gcol = lax.axis_size("gcol")
    blocks = n_grow * n_gcol
    _, bands_all, planes, merged = valence.shape
    pairs = pair_bands.size
    row_count = g_index.size // (n_pair * blocks)
    col_count = slab_index.size // (n_pair * blocks)
    if (planes, pairs, n_pair, pair_bands.shape[0], row_count + col_count) != (8, 32, 2, 1, BLOCK_ROWS):
        return on_device_general(valence, conduction, pair_bands, e_val, e_cond, g_index, slab_index)
    rows = g_index.reshape(n_pair, n_grow, n_gcol, -1).transpose(1, 2, 0, 3)
    cols = slab_index.reshape(n_gcol, n_pair, n_grow, -1).transpose(2, 0, 1, 3)
    points = jnp.concatenate([rows, cols], axis=3).reshape(blocks, -1)
    lanes = pairs * planes
    half = BLOCK_ROWS // 2
    width = 4 * pairs
    vmem = pl.BlockSpec(memory_space=pltpu.VMEM)
    smem = pl.BlockSpec(memory_space=pltpu.SMEM)
    sem = pltpu.SemaphoreType.DMA
    bf16 = jnp.bfloat16
    return pl.pallas_call(
        functools.partial(slab_kernel, (n_pair, n_grow, n_gcol), row_count),
        out_shape=jax.ShapeDtypeStruct(
            (2, n_gcol * row_count, n_pair * n_grow * col_count), jnp.float32
        ),
        in_specs=[smem, smem, smem, pl.BlockSpec(memory_space=pl.ANY), vmem, vmem, vmem],
        out_specs=vmem,
        scratch_shapes=[
            *[pltpu.VMEM((2, bands_all, planes, CHUNK * NGRID), bf16)] * SLOTS,
            pltpu.VMEM((lanes // 128, 2 * NGRID * PITCH, 128), jnp.float32),
            pltpu.VMEM((2 * NGRID, NGRID, lanes), bf16),
            pltpu.VMEM((4 * lanes, width), bf16),
            pltpu.VMEM((NGRID, 2 * lanes), bf16),
            pltpu.VMEM((blocks, BLOCK_ROWS, width), bf16),
            pltpu.VMEM((blocks, BLOCK_ROWS, width), bf16),
            pltpu.VMEM((n_pair, half, width), bf16),
            pltpu.VMEM((n_pair * n_gcol, half, width), bf16),
            pltpu.VMEM((n_pair * col_count, width), bf16),
            pltpu.VMEM((n_pair * n_grow, n_pair * col_count, width), bf16),
            sem((SLOTS,)),
            sem((blocks,)), sem((blocks,)),
            sem((n_pair * n_gcol,)), sem((n_pair * n_gcol,)),
            sem((n_pair * n_grow,)), sem((n_pair * n_grow,)),
        ],
        compiler_params=pltpu.CompilerParams(
            collective_id=0, has_side_effects=True, vmem_limit_bytes=52 * 2**20
        ),
        name="slab",
    )(pair_bands.reshape(-1), e_val, e_cond, valence, conduction, points, jnp.asarray(fixed_table()))


def solution(mesh):
    in_specs = (
        P(None, None, ("grow", "gcol"), None),
        P(None, "pair", ("grow", "gcol"), None),
        P("pair", None),
        P(),
        P("pair"),
        P(),
        P(),
    )
    out_specs = P(None, ("pair", "grow"), "gcol")
    return jax.shard_map(
        on_device, mesh=mesh, in_specs=in_specs, out_specs=out_specs, check_vma=False
    )
```

```python
import functools
import math

import jax
import jax.numpy as jnp
import numpy as np
from jax import lax
from jax.experimental import pallas as pl
from jax.experimental.pallas import tpu as pltpu
from jax.sharding import PartitionSpec as P

NGRID = 128


def transform_table(count, positions):
    freq = jnp.arange(count, dtype=jnp.int32)
    phase = freq[:, None] * positions[None, :] % count
    angle = phase.astype(jnp.float32) * (2.0 * math.pi / count)
    scale = 1.0 / math.sqrt(count)
    cosine = (jnp.cos(angle) * scale).astype(jnp.bfloat16)
    sine = (jnp.sin(angle) * scale).astype(jnp.bfloat16)
    upper = jnp.stack([cosine, sine], axis=1)
    lower = jnp.stack([-sine, cosine], axis=1)
    return jnp.stack([upper, lower])


def on_device_general(valence, conduction, pair_bands, e_val, e_cond, g_index, slab_index):
    n_pair = lax.axis_size("pair")
    n_grow = lax.axis_size("grow")
    n_gcol = lax.axis_size("gcol")
    grow_at = lax.axis_index("grow")
    gcol_at = lax.axis_index("gcol")
    planes = valence.shape[2]
    bands_here, partners = pair_bands.shape
    pairs_here = bands_here * partners
    total_pairs = pairs_here * n_pair
    picked = jnp.take(valence, pair_bands.reshape(-1), axis=1).astype(jnp.float32)
    cond_rep = jnp.repeat(conduction, partners, axis=1).astype(jnp.float32)
    real_part = picked[0] * cond_rep[0] + picked[1] * cond_rep[1]
    imag_part = picked[0] * cond_rep[1] - picked[1] * cond_rep[0]
    density = jnp.stack([real_part, imag_part]).astype(jnp.bfloat16)
    density = jnp.transpose(density.reshape(2, pairs_here, planes, NGRID, NGRID), (0, 2, 3, 4, 1))
    natural = transform_table(NGRID, jnp.arange(NGRID, dtype=jnp.int32))
    third = jnp.einsum(
        "okix,iabxp->oabkp", natural, density, preferred_element_type=jnp.float32
    ).astype(jnp.bfloat16)
    second = jnp.einsum(
        "okix,iaxbp->oakbp", natural, third, preferred_element_type=jnp.float32
    ).astype(jnp.bfloat16)
    moved = lax.all_to_all(second, ("grow", "gcol"), split_axis=3, concat_axis=1, tiled=True)
    positions = jnp.arange(NGRID, dtype=jnp.int32)
    wide_two = NGRID
    base_three = (grow_at * n_gcol + gcol_at) * planes
    table_first = transform_table(NGRID, positions)
    elements = jnp.einsum(
        "okix,ixabp->okabp", table_first, moved, preferred_element_type=jnp.float32
    ).astype(jnp.bfloat16)
    flat = elements.reshape(2, -1, pairs_here)

    def local_offset(index):
        first_q = index // (NGRID * NGRID)
        second_q = index // NGRID % NGRID
        third_q = index % NGRID
        return (first_q * wide_two + second_q) * planes + third_q - base_three

    row_count = g_index.shape[0] // (n_pair * n_grow * n_gcol)
    row_ids = g_index.reshape(n_pair, n_grow, n_gcol, row_count)[:, grow_at, gcol_at]
    rows = jnp.take(flat, local_offset(row_ids).reshape(-1), axis=1).reshape(
        2, n_pair, row_count, pairs_here
    )
    gaps = jnp.take(e_val, pair_bands) - e_cond[:, None]
    weight = (2.0 / (gaps * math.sqrt(total_pairs))).reshape(-1)
    weighted = (rows.astype(jnp.float32) * weight).astype(jnp.bfloat16)
    col_count = slab_index.shape[0] // (n_pair * n_grow * n_gcol)
    col_ids = slab_index.reshape(n_gcol, n_pair, n_grow, col_count)[gcol_at, :, grow_at]
    cols = jnp.take(flat, local_offset(col_ids).reshape(-1), axis=1).reshape(
        2, n_pair, col_count, pairs_here
    )
    row_block = lax.all_to_all(weighted, "pair", split_axis=1, concat_axis=3, tiled=True).reshape(
        2, row_count, total_pairs
    )
    spread = lax.all_gather(
        cols.reshape(2, n_pair, 1, col_count, pairs_here), "grow", axis=2, tiled=True
    )
    slab = lax.all_gather(spread, "pair", axis=4, tiled=True).reshape(2, -1, total_pairs)
    conjugate = jnp.stack([jnp.stack([slab[0], slab[1]]), jnp.stack([-slab[1], slab[0]])])
    return jnp.einsum(
        "irk,oick->orc",
        lax.all_gather(row_block, "gcol", axis=1, tiled=True),
        conjugate,
        preferred_element_type=jnp.float32,
    )


CHUNK = 16
PITCH = 17
SLOTS = 3
BLOCK_ROWS = 128
MESH = pl.DeviceIdType.MESH


def slab_kernel(
    sizes, row_count, bands_in, e_val_in, e_cond, val, cond_in, g_rows_in, slab_rows_in, t3_in, out,
    bands, e_val, cond, g_rows, slab_rows, t3,
    slot_a, slot_b, slot_c, stage_a, stage_b, third, pack, spread, sums, inbox, row_out, row_in, col_out, col_in,
    sems, load_sems, sum_send, sum_recv, row_send, row_recv, col_send, col_recv,
):
    n_pair, n_grow, n_gcol = sizes
    blocks = n_grow * n_gcol
    pair_at = lax.axis_index("pair")
    grow_at = lax.axis_index("grow")
    gcol_at = lax.axis_index("gcol")
    me = grow_at * n_gcol + gcol_at
    half = BLOCK_ROWS // 2
    col_count = BLOCK_ROWS - row_count
    pairs = bands.shape[1]
    stages = (stage_a, stage_b)
    held = (slot_a, slot_b, slot_c)
    slots = len(held)
    planes, wide = slot_a.shape[2], slot_a.shape[3]
    lanes = pairs * planes
    chunks = NGRID // CHUNK

    def place(pair, grow, gcol):
        return {"pair": pair, "grow": grow, "gcol": gcol}

    def arrival(src, dst, send, recv):
        at = place(lax.rem(pair_at + 1, n_pair), grow_at, gcol_at)
        return pltpu.make_async_remote_copy(
            src_ref=src, dst_ref=dst, send_sem=send, recv_sem=recv, device_id=at, device_id_type=MESH
        )

    def block_place(distance):
        other = lax.rem(me + distance, blocks)
        return other, place(pair_at, other // n_gcol, lax.rem(other, n_gcol))

    def fetch(chunk):
        return pltpu.make_async_copy(
            val.at[:, :, :, pl.ds(chunk * wide, wide)], held[chunk % slots], sems.at[chunk % slots]
        )

    loads = [
        pltpu.make_async_copy(src, dst, load_sems.at[number])
        for number, (src, dst) in enumerate(
            ((bands_in, bands), (e_val_in, e_val), (t3_in, t3), (cond_in, cond), (g_rows_in, g_rows), (slab_rows_in, slab_rows))
        )
    ]
    for load in loads:
        load.start()
    for chunk in range(slots - 1):
        fetch(chunk).start()

    barrier = pltpu.get_barrier_semaphore()
    greeted = 0
    for distance in range(1, blocks):
        pl.semaphore_signal(barrier, inc=1, device_id=block_place(distance)[1], device_id_type=MESH)
        greeted += 1
    for far in range(1, n_pair):
        other = lax.rem(pair_at + far, n_pair)
        for step in range(n_gcol):
            at = place(other, grow_at, lax.rem(gcol_at + step, n_gcol))
            pl.semaphore_signal(barrier, inc=1, device_id=at, device_id_type=MESH)
            greeted += 1
        for step in range(1, n_grow):
            at = place(other, lax.rem(grow_at + step, n_grow), gcol_at)
            pl.semaphore_signal(barrier, inc=1, device_id=at, device_id_type=MESH)
            greeted += 1

    for load in loads:
        load.wait()
    source = lax.broadcasted_iota(jnp.int32, pack.shape, 0)
    target = source // lanes * pairs + source % lanes // planes
    pack[...] = jnp.where(
        target == lax.broadcasted_iota(jnp.int32, pack.shape, 1), 1.0, 0.0
    ).astype(jnp.bfloat16)
    plane = lax.broadcasted_iota(jnp.int32, (NGRID, lanes), 1) % planes + me * planes
    expand = jnp.where(
        lax.broadcasted_iota(jnp.int32, (NGRID, lanes), 0) == plane, 1.0, 0.0
    ).astype(jnp.bfloat16)
    for part in range(2):
        spread[:, part * lanes : (part + 1) * lanes] = jnp.dot(
            t3[:NGRID, part * NGRID : (part + 1) * NGRID], expand, preferred_element_type=jnp.float32
        ).astype(jnp.bfloat16)
    spot_of = lax.broadcasted_iota(jnp.int32, (1, 4 * pairs), 1) % pairs
    energy = jnp.zeros((1, 4 * pairs), jnp.float32)
    for pair in range(pairs):
        energy = jnp.where(spot_of == pair, e_val[bands[0, pair]], energy)
    weight = 2.0 / ((energy - e_cond[0]) * math.sqrt(pairs * n_pair))

    groups = 2 * NGRID // 8 // CHUNK

    def settle(chunk, group):
        for inner in range(8):
            start = pl.multiple_of(group * (8 * PITCH), 8) + inner * PITCH
            for part in range(lanes // 128):
                third[group * 8 + inner, chunk * CHUNK : (chunk + 1) * CHUNK, part * 128 : (part + 1) * 128] = (
                    stages[chunk % 2][part, pl.ds(start, CHUNK), :].astype(jnp.bfloat16)
                )

    for chunk in range(chunks):
        slot = held[chunk % slots]
        fetch(chunk).wait()
        if chunk + slots - 1 < chunks:
            fetch(chunk + slots - 1).start()

        @pl.loop(0, CHUNK, unroll=4)
        def _(step):
            there = pl.ds(pl.multiple_of(chunk * wide + step * NGRID, NGRID), NGRID)
            here = pl.ds(pl.multiple_of(step * NGRID, NGRID), NGRID)
            c_re = cond[0, 0, :, there].astype(jnp.float32)
            c_im = cond[1, 0, :, there].astype(jnp.float32)
            reals, imags = [], []
            for pair in range(pairs):
                v_re = slot[0, bands[0, pair], :, here].astype(jnp.float32)
                v_im = slot[1, bands[0, pair], :, here].astype(jnp.float32)
                reals.append(v_re * c_re + v_im * c_im)
                imags.append(v_re * c_im - v_im * c_re)
            density = jnp.concatenate(
                [jnp.concatenate(reals, axis=0), jnp.concatenate(imags, axis=0)], axis=1
            ).astype(jnp.bfloat16)
            moved = lax.dot_general(
                t3[...], density, (((1,), (1,)), ((), ())), preferred_element_type=jnp.float32
            )
            for part in range(lanes // 128):
                stages[chunk % 2][part, pl.ds(step, 2 * NGRID, stride=PITCH), :] = moved[
                    :, part * 128 : (part + 1) * 128
                ]

            if chunk:
                for group in range(groups):
                    settle(chunk - 1, step * groups + group)

    @pl.loop(0, 2 * NGRID // 8)
    def _(group):
        settle(chunks - 1, group)

    width = NGRID // blocks
    wide_two = NGRID // n_gcol
    count = n_pair * BLOCK_ROWS
    across = lax.broadcasted_iota(jnp.int32, (1, BLOCK_ROWS), 1)

    def listed_points(block):
        grow, gcol = block // n_gcol, lax.rem(block, n_gcol)
        found = []
        for pair in range(n_pair):
            start = ((pair * n_grow + grow) * n_gcol + gcol) * row_count
            line, offset = start // 128, lax.rem(start, 128)
            back = lax.rem(128 - offset, 128)
            split = 128 - offset
            here = pltpu.roll(g_rows[pl.ds(line, 1), :], back, 1)
            after = pltpu.roll(g_rows[pl.ds(lax.rem(line + 1, g_rows.shape[0]), 1), :], back, 1)
            start = ((gcol * n_pair + pair) * n_grow + grow) * col_count
            line, offset = start // 128, lax.rem(start, 128)
            cols = pltpu.roll(
                slab_rows[pl.ds(line, 1), :], lax.rem(row_count + 128 - offset, 128), 1
            )
            rows = jnp.where(across < split, here, after)
            found.append(jnp.where(across < row_count, rows, cols))
        return jnp.concatenate(found, axis=1)

    def partial_sums(block):
        first_row = pl.multiple_of(lax.rem(block, n_gcol) * wide_two, wide_two)
        table = jnp.concatenate(
            [t3[pl.ds(first_row, wide_two), :], t3[pl.ds(first_row + NGRID, wide_two), :]], axis=0
        )
        reals, imags = [], []
        for inner in range(width):
            freq = block * width + inner
            field = jnp.concatenate([third[freq], third[NGRID + freq]], axis=0)
            moved = jnp.dot(table, field, preferred_element_type=jnp.float32).astype(jnp.bfloat16)
            reals.append(moved[:wide_two])
            imags.append(moved[wide_two:])
        listed = listed_points(block)
        spot = (listed & (width - 1)) * wide_two + ((listed >> 7) & (wide_two - 1))
        chosen = jnp.where(
            lax.broadcasted_iota(jnp.int32, (width * wide_two, count), 0) == spot, 1.0, 0.0
        ).astype(jnp.bfloat16)
        wave = jnp.where(
            lax.broadcasted_iota(jnp.int32, (NGRID, count), 0) == (listed >> 14), 1.0, 0.0
        ).astype(jnp.bfloat16)

        def choose(mask, field):
            return lax.dot_general(
                mask, field, (((0,), (0,)), ((), ())), preferred_element_type=jnp.float32
            )

        re = choose(chosen, jnp.concatenate(reals, axis=0))
        im = choose(chosen, jnp.concatenate(imags, axis=0))
        both = choose(wave, spread[...])
        cosine, sine = both[:, :lanes], both[:, lanes:]
        z_re = (cosine * re + sine * im).astype(jnp.bfloat16)
        z_im = (cosine * im - sine * re).astype(jnp.bfloat16)
        parts = []
        for low in range(0, BLOCK_ROWS, half):
            for z in (z_re, z_im):
                starts = range(low, count, BLOCK_ROWS)
                parts.append(jnp.concatenate([z[at : at + half] for at in starts], axis=0))
        return jnp.dot(
            jnp.concatenate(parts, axis=1), pack[...], preferred_element_type=jnp.float32
        )

    def sum_copy(distance):
        other, at = block_place(distance)
        return pltpu.make_async_remote_copy(
            src_ref=sums.at[distance], dst_ref=inbox.at[distance],
            send_sem=sum_send.at[distance], recv_sem=sum_recv.at[distance],
            device_id=at, device_id_type=MESH,
        )

    pl.semaphore_wait(barrier, greeted)

    @pl.loop(1, blocks, unroll=3)
    def _(distance):
        sums[distance] = partial_sums(lax.rem(me + distance, blocks)).astype(jnp.bfloat16)
        sum_copy(distance).start()

    total = partial_sums(me)
    for distance in range(1, blocks):
        sum_copy(distance).wait_recv()
        total = total + inbox[distance].astype(jnp.float32)
    elements = total.astype(jnp.bfloat16).astype(jnp.float32)
    weighted = (elements * weight).astype(jnp.bfloat16)
    cols = [elements[(one + 1) * half - col_count : (one + 1) * half] for one in range(n_pair)]
    cols = jnp.concatenate(cols, axis=0).astype(jnp.bfloat16)
    col_out[...] = cols
    for one in range(n_pair):
        row_out[one] = weighted[one * half : (one + 1) * half]
    row_slot = pair_at * n_gcol + gcol_at
    col_slot = pair_at * n_grow + grow_at
    row_copies, col_copies = [], []
    for far in range(n_pair):
        other = lax.rem(pair_at + far, n_pair)
        behind = lax.rem(pair_at + n_pair - far, n_pair)
        for step in range(n_grow):
            if far or step:
                number = far * n_grow + step
                copy = pltpu.make_async_remote_copy(
                    src_ref=col_out, dst_ref=col_in.at[col_slot],
                    send_sem=col_send.at[number], recv_sem=col_recv.at[col_slot],
                    device_id=place(other, lax.rem(grow_at + step, n_grow), gcol_at),
                    device_id_type=MESH,
                )
                copy.start()
                source = behind * n_grow + lax.rem(grow_at + n_grow - step, n_grow)
                col_copies.append((copy, source))
        for step in range(n_gcol):
            if far or step:
                number = far * n_gcol + step
                copy = pltpu.make_async_remote_copy(
                    src_ref=row_out.at[other], dst_ref=row_in.at[row_slot],
                    send_sem=row_send.at[number], recv_sem=row_recv.at[row_slot],
                    device_id=place(other, grow_at, lax.rem(gcol_at + step, n_gcol)),
                    device_id_type=MESH,
                )
                copy.start()
                source = behind * n_gcol + lax.rem(gcol_at + n_gcol - step, n_gcol)
                row_copies.append((copy, source))
    col_in[col_slot] = cols
    row_in[row_slot] = row_out[pair_at]
    for _, source in col_copies:
        arrival(col_out, col_in.at[source], col_send.at[0], col_recv.at[source]).wait_recv()
    lane = lax.broadcasted_iota(jnp.int32, (out.shape[2], 4 * pairs), 1)
    tables = {}
    for one in range(n_pair):
        pieces = []
        for target in range(n_pair):
            for grow in range(n_grow):
                piece = col_in[one * n_grow + grow].astype(jnp.float32)
                pieces.append(piece[target * col_count : (target + 1) * col_count])
        straight = jnp.where(lane >= 2 * pairs, jnp.concatenate(pieces, axis=0), 0.0)
        crossed = jnp.where(
            lane >= 3 * pairs,
            pltpu.roll(straight, pairs, 1),
            jnp.where(lane >= 2 * pairs, -pltpu.roll(straight, 3 * pairs, 1), 0.0),
        )
        for part, table in enumerate((straight, crossed)):
            tables[one, 1, part] = table.astype(jnp.bfloat16)
            tables[one, 0, part] = pltpu.roll(table, 2 * pairs, 1).astype(jnp.bfloat16)
    for _, source in row_copies:
        arrival(row_out.at[0], row_in.at[source], row_send.at[0], row_recv.at[source]).wait_recv()
    rows = [
        jnp.concatenate([row_in[one * n_gcol + gcol] for gcol in range(n_gcol)], axis=0)
        for one in range(n_pair)
    ]
    rows = jnp.concatenate(rows, axis=1)
    for low in range(2):
        for part in range(2):
            table = jnp.concatenate([tables[one, low, part] for one in range(n_pair)], axis=1)
            made = lax.dot_general(
                rows, table, (((1,), (1,)), ((), ())), preferred_element_type=jnp.float32
            )
            kept = min(half, row_count - low * half)
            for gcol in range(n_gcol):
                start = gcol * row_count + low * half
                out[part, start : start + kept, :] = made[gcol * half : gcol * half + kept]
    for distance in range(1, blocks):
        sum_copy(distance).wait_send()
    for copy, _ in col_copies + row_copies:
        copy.wait_send()


def fixed_table():
    freq = np.arange(NGRID, dtype=np.int32)
    angle = (freq[:, None] * freq[None, :] % NGRID).astype(np.float32) * np.float32(2.0 * math.pi / NGRID)
    scale = np.float32(1.0 / math.sqrt(NGRID))
    cosine = np.cos(angle) * scale
    sine = np.sin(angle) * scale
    return np.block([[cosine, sine], [-sine, cosine]]).astype(jnp.bfloat16)


def on_device(valence, conduction, pair_bands, e_val, e_cond, g_index, slab_index):
    n_pair = lax.axis_size("pair")
    n_grow = lax.axis_size("grow")
    n_gcol = lax.axis_size("gcol")
    blocks = n_grow * n_gcol
    _, bands_all, planes, merged = valence.shape
    pairs = pair_bands.size
    row_count = g_index.size // (n_pair * blocks)
    col_count = slab_index.size // (n_pair * blocks)
    if (planes, pairs, n_pair, pair_bands.shape[0], row_count + col_count) != (8, 32, 2, 1, BLOCK_ROWS):
        return on_device_general(valence, conduction, pair_bands, e_val, e_cond, g_index, slab_index)
    lanes = pairs * planes
    half = BLOCK_ROWS // 2
    width = 4 * pairs
    vmem = pl.BlockSpec(memory_space=pltpu.VMEM)
    smem = pl.BlockSpec(memory_space=pltpu.SMEM)
    hbm = pl.BlockSpec(memory_space=pltpu.HBM)
    sem = pltpu.SemaphoreType.DMA
    bf16 = jnp.bfloat16
    return pl.pallas_call(
        functools.partial(slab_kernel, (n_pair, n_grow, n_gcol), row_count),
        out_shape=jax.ShapeDtypeStruct(
            (2, n_gcol * row_count, n_pair * n_grow * col_count), jnp.float32
        ),
        in_specs=[hbm, hbm, smem, hbm, hbm, hbm, hbm, hbm],
        out_specs=vmem,
        scratch_shapes=[
            pltpu.SMEM(pair_bands.shape, jnp.int32),
            pltpu.SMEM(e_val.shape, jnp.float32),
            pltpu.VMEM(conduction.shape, bf16),
            pltpu.VMEM((g_index.size // 128, 128), jnp.int32),
            pltpu.VMEM((slab_index.size // 128, 128), jnp.int32),
            pltpu.VMEM((2 * NGRID, 2 * NGRID), bf16),
            *[pltpu.VMEM((2, bands_all, planes, CHUNK * NGRID), bf16)] * SLOTS,
            *[pltpu.VMEM((lanes // 128, 2 * NGRID * PITCH, 128), jnp.float32)] * 2,
            pltpu.VMEM((2 * NGRID, NGRID, lanes), bf16),
            pltpu.VMEM((4 * lanes, width), bf16),
            pltpu.VMEM((NGRID, 2 * lanes), bf16),
            pltpu.VMEM((blocks, BLOCK_ROWS, width), bf16),
            pltpu.VMEM((blocks, BLOCK_ROWS, width), bf16),
            pltpu.VMEM((n_pair, half, width), bf16),
            pltpu.VMEM((n_pair * n_gcol, half, width), bf16),
            pltpu.VMEM((n_pair * col_count, width), bf16),
            pltpu.VMEM((n_pair * n_grow, n_pair * col_count, width), bf16),
            sem((SLOTS,)),
            sem((6,)),
            sem((blocks,)), sem((blocks,)),
            sem((n_pair * n_gcol,)), sem((n_pair * n_gcol,)),
            sem((n_pair * n_grow,)), sem((n_pair * n_grow,)),
        ],
        compiler_params=pltpu.CompilerParams(
            collective_id=0, has_side_effects=True, vmem_limit_bytes=56 * 2**20
        ),
        name="slab",
    )(
        pair_bands, e_val, e_cond, valence, conduction,
        g_index.reshape(-1, 128), slab_index.reshape(-1, 128), jnp.asarray(fixed_table()),
    )


def solution(mesh):
    in_specs = (
        P(None, None, ("grow", "gcol"), None),
        P(None, "pair", ("grow", "gcol"), None),
        P("pair", None),
        P(),
        P("pair"),
        P(),
        P(),
    )
    out_specs = P(None, ("pair", "grow"), "gcol")
    return jax.shard_map(
        on_device, mesh=mesh, in_specs=in_specs, out_specs=out_specs, check_vma=False
    )
```

```python
import functools
import math

import jax
import jax.numpy as jnp
import numpy as np
from jax import lax
from jax.experimental import pallas as pl
from jax.experimental.pallas import tpu as pltpu
from jax.sharding import PartitionSpec as P

NGRID = 128


def transform_table(count, positions):
    freq = jnp.arange(count, dtype=jnp.int32)
    phase = freq[:, None] * positions[None, :] % count
    angle = phase.astype(jnp.float32) * (2.0 * math.pi / count)
    scale = 1.0 / math.sqrt(count)
    cosine = (jnp.cos(angle) * scale).astype(jnp.bfloat16)
    sine = (jnp.sin(angle) * scale).astype(jnp.bfloat16)
    upper = jnp.stack([cosine, sine], axis=1)
    lower = jnp.stack([-sine, cosine], axis=1)
    return jnp.stack([upper, lower])


def on_device_general(valence, conduction, pair_bands, e_val, e_cond, g_index, slab_index):
    n_pair = lax.axis_size("pair")
    n_grow = lax.axis_size("grow")
    n_gcol = lax.axis_size("gcol")
    grow_at = lax.axis_index("grow")
    gcol_at = lax.axis_index("gcol")
    planes = valence.shape[2]
    bands_here, partners = pair_bands.shape
    pairs_here = bands_here * partners
    total_pairs = pairs_here * n_pair
    picked = jnp.take(valence, pair_bands.reshape(-1), axis=1).astype(jnp.float32)
    cond_rep = jnp.repeat(conduction, partners, axis=1).astype(jnp.float32)
    real_part = picked[0] * cond_rep[0] + picked[1] * cond_rep[1]
    imag_part = picked[0] * cond_rep[1] - picked[1] * cond_rep[0]
    density = jnp.stack([real_part, imag_part]).astype(jnp.bfloat16)
    density = jnp.transpose(density.reshape(2, pairs_here, planes, NGRID, NGRID), (0, 2, 3, 4, 1))
    natural = transform_table(NGRID, jnp.arange(NGRID, dtype=jnp.int32))
    third = jnp.einsum(
        "okix,iabxp->oabkp", natural, density, preferred_element_type=jnp.float32
    ).astype(jnp.bfloat16)
    second = jnp.einsum(
        "okix,iaxbp->oakbp", natural, third, preferred_element_type=jnp.float32
    ).astype(jnp.bfloat16)
    moved = lax.all_to_all(second, ("grow", "gcol"), split_axis=3, concat_axis=1, tiled=True)
    positions = jnp.arange(NGRID, dtype=jnp.int32)
    wide_two = NGRID
    base_three = (grow_at * n_gcol + gcol_at) * planes
    table_first = transform_table(NGRID, positions)
    elements = jnp.einsum(
        "okix,ixabp->okabp", table_first, moved, preferred_element_type=jnp.float32
    ).astype(jnp.bfloat16)
    flat = elements.reshape(2, -1, pairs_here)

    def local_offset(index):
        first_q = index // (NGRID * NGRID)
        second_q = index // NGRID % NGRID
        third_q = index % NGRID
        return (first_q * wide_two + second_q) * planes + third_q - base_three

    row_count = g_index.shape[0] // (n_pair * n_grow * n_gcol)
    row_ids = g_index.reshape(n_pair, n_grow, n_gcol, row_count)[:, grow_at, gcol_at]
    rows = jnp.take(flat, local_offset(row_ids).reshape(-1), axis=1).reshape(
        2, n_pair, row_count, pairs_here
    )
    gaps = jnp.take(e_val, pair_bands) - e_cond[:, None]
    weight = (2.0 / (gaps * math.sqrt(total_pairs))).reshape(-1)
    weighted = (rows.astype(jnp.float32) * weight).astype(jnp.bfloat16)
    col_count = slab_index.shape[0] // (n_pair * n_grow * n_gcol)
    col_ids = slab_index.reshape(n_gcol, n_pair, n_grow, col_count)[gcol_at, :, grow_at]
    cols = jnp.take(flat, local_offset(col_ids).reshape(-1), axis=1).reshape(
        2, n_pair, col_count, pairs_here
    )
    row_block = lax.all_to_all(weighted, "pair", split_axis=1, concat_axis=3, tiled=True).reshape(
        2, row_count, total_pairs
    )
    spread = lax.all_gather(
        cols.reshape(2, n_pair, 1, col_count, pairs_here), "grow", axis=2, tiled=True
    )
    slab = lax.all_gather(spread, "pair", axis=4, tiled=True).reshape(2, -1, total_pairs)
    conjugate = jnp.stack([jnp.stack([slab[0], slab[1]]), jnp.stack([-slab[1], slab[0]])])
    return jnp.einsum(
        "irk,oick->orc",
        lax.all_gather(row_block, "gcol", axis=1, tiled=True),
        conjugate,
        preferred_element_type=jnp.float32,
    )


CHUNK = 16
PITCH = 17
SLOTS = 3
BLOCK_ROWS = 128
MESH = pl.DeviceIdType.MESH


def slab_kernel(
    sizes, row_count, bands_in, e_val_in, e_cond, val, cond_in, g_rows_in, slab_rows_in, t3_in, out,
    bands, e_val, cond, g_rows, slab_rows, t3,
    slot_a, slot_b, slot_c, stage_a, stage_b, third, pack, spread, sums, inbox, row_out, row_in, col_out, col_in,
    sems, load_sems, sum_send, sum_recv, row_send, row_recv, col_send, col_recv,
):
    n_pair, n_grow, n_gcol = sizes
    blocks = n_grow * n_gcol
    pair_at = lax.axis_index("pair")
    grow_at = lax.axis_index("grow")
    gcol_at = lax.axis_index("gcol")
    me = grow_at * n_gcol + gcol_at
    half = BLOCK_ROWS // 2
    col_count = BLOCK_ROWS - row_count
    pairs = bands.shape[1]
    stages = (stage_a, stage_b)
    held = (slot_a, slot_b, slot_c)
    slots = len(held)
    planes, wide = slot_a.shape[2], slot_a.shape[3]
    lanes = pairs * planes
    chunks = NGRID // CHUNK

    def place(pair, grow, gcol):
        return {"pair": pair, "grow": grow, "gcol": gcol}

    def arrival(src, dst, send, recv):
        at = place(lax.rem(pair_at + 1, n_pair), grow_at, gcol_at)
        return pltpu.make_async_remote_copy(
            src_ref=src, dst_ref=dst, send_sem=send, recv_sem=recv, device_id=at, device_id_type=MESH
        )

    def block_place(distance):
        other = lax.rem(me + distance, blocks)
        return other, place(pair_at, other // n_gcol, lax.rem(other, n_gcol))

    def fetch(chunk):
        return pltpu.make_async_copy(
            val.at[:, :, :, pl.ds(chunk * wide, wide)], held[chunk % slots], sems.at[chunk % slots]
        )

    loads = [
        pltpu.make_async_copy(src, dst, load_sems.at[number])
        for number, (src, dst) in enumerate(
            ((bands_in, bands), (e_val_in, e_val), (t3_in, t3), (cond_in, cond), (g_rows_in, g_rows), (slab_rows_in, slab_rows))
        )
    ]
    for load in loads:
        load.start()
    for chunk in range(slots - 1):
        fetch(chunk).start()

    barrier = pltpu.get_barrier_semaphore()
    greeted = 0
    for distance in range(1, blocks):
        pl.semaphore_signal(barrier, inc=1, device_id=block_place(distance)[1], device_id_type=MESH)
        greeted += 1
    for far in range(1, n_pair):
        other = lax.rem(pair_at + far, n_pair)
        for step in range(n_gcol):
            at = place(other, grow_at, lax.rem(gcol_at + step, n_gcol))
            pl.semaphore_signal(barrier, inc=1, device_id=at, device_id_type=MESH)
            greeted += 1
        for step in range(1, n_grow):
            at = place(other, lax.rem(grow_at + step, n_grow), gcol_at)
            pl.semaphore_signal(barrier, inc=1, device_id=at, device_id_type=MESH)
            greeted += 1

    for load in loads:
        load.wait()
    source = lax.broadcasted_iota(jnp.int32, pack.shape, 0)
    target = source // lanes * pairs + source % lanes // planes
    pack[...] = jnp.where(
        target == lax.broadcasted_iota(jnp.int32, pack.shape, 1), 1.0, 0.0
    ).astype(jnp.bfloat16)
    plane = lax.broadcasted_iota(jnp.int32, (NGRID, lanes), 1) % planes + me * planes
    expand = jnp.where(
        lax.broadcasted_iota(jnp.int32, (NGRID, lanes), 0) == plane, 1.0, 0.0
    ).astype(jnp.bfloat16)
    for part in range(2):
        spread[:, part * lanes : (part + 1) * lanes] = jnp.dot(
            t3[:NGRID, part * NGRID : (part + 1) * NGRID], expand, preferred_element_type=jnp.float32
        ).astype(jnp.bfloat16)
    spot_of = lax.broadcasted_iota(jnp.int32, (1, 4 * pairs), 1) % pairs
    energy = jnp.zeros((1, 4 * pairs), jnp.float32)
    for pair in range(pairs):
        energy = jnp.where(spot_of == pair, e_val[bands[0, pair]], energy)
    weight = 2.0 / ((energy - e_cond[0]) * math.sqrt(pairs * n_pair))

    groups = 2 * NGRID // 8 // CHUNK

    def settle(chunk, group):
        for inner in range(8):
            start = pl.multiple_of(group * (8 * PITCH), 8) + inner * PITCH
            for part in range(lanes // 128):
                third[group * 8 + inner, chunk * CHUNK : (chunk + 1) * CHUNK, part * 128 : (part + 1) * 128] = (
                    stages[chunk % 2][part, pl.ds(start, CHUNK), :].astype(jnp.bfloat16)
                )

    for chunk in range(chunks):
        slot = held[chunk % slots]
        fetch(chunk).wait()
        if chunk + slots - 1 < chunks:
            fetch(chunk + slots - 1).start()

        @pl.loop(0, CHUNK, unroll=8)
        def _(step):
            there = pl.ds(pl.multiple_of(chunk * wide + step * NGRID, NGRID), NGRID)
            here = pl.ds(pl.multiple_of(step * NGRID, NGRID), NGRID)
            c_re = cond[0, 0, :, there].astype(jnp.float32)
            c_im = cond[1, 0, :, there].astype(jnp.float32)
            reals, imags = [], []
            for pair in range(pairs):
                v_re = slot[0, bands[0, pair], :, here].astype(jnp.float32)
                v_im = slot[1, bands[0, pair], :, here].astype(jnp.float32)
                reals.append(v_re * c_re + v_im * c_im)
                imags.append(v_re * c_im - v_im * c_re)
            density = jnp.concatenate(
                [jnp.concatenate(reals, axis=0), jnp.concatenate(imags, axis=0)], axis=1
            ).astype(jnp.bfloat16)
            moved = lax.dot_general(
                t3[...], density, (((1,), (1,)), ((), ())), preferred_element_type=jnp.float32
            )
            for part in range(lanes // 128):
                stages[chunk % 2][part, pl.ds(step, 2 * NGRID, stride=PITCH), :] = moved[
                    :, part * 128 : (part + 1) * 128
                ]

            if chunk:
                for group in range(groups):
                    settle(chunk - 1, step * groups + group)

    @pl.loop(0, 2 * NGRID // 8)
    def _(group):
        settle(chunks - 1, group)

    width = NGRID // blocks
    wide_two = NGRID // n_gcol
    count = n_pair * BLOCK_ROWS
    across = lax.broadcasted_iota(jnp.int32, (1, BLOCK_ROWS), 1)

    def listed_points(block):
        grow, gcol = block // n_gcol, lax.rem(block, n_gcol)
        found = []
        for pair in range(n_pair):
            start = ((pair * n_grow + grow) * n_gcol + gcol) * row_count
            line, offset = start // 128, lax.rem(start, 128)
            back = lax.rem(128 - offset, 128)
            split = 128 - offset
            here = pltpu.roll(g_rows[pl.ds(line, 1), :], back, 1)
            after = pltpu.roll(g_rows[pl.ds(lax.rem(line + 1, g_rows.shape[0]), 1), :], back, 1)
            start = ((gcol * n_pair + pair) * n_grow + grow) * col_count
            line, offset = start // 128, lax.rem(start, 128)
            cols = pltpu.roll(
                slab_rows[pl.ds(line, 1), :], lax.rem(row_count + 128 - offset, 128), 1
            )
            rows = jnp.where(across < split, here, after)
            found.append(jnp.where(across < row_count, rows, cols))
        return jnp.concatenate(found, axis=1)

    def partial_sums(block):
        first_row = pl.multiple_of(lax.rem(block, n_gcol) * wide_two, wide_two)
        table = jnp.concatenate(
            [t3[pl.ds(first_row, wide_two), :], t3[pl.ds(first_row + NGRID, wide_two), :]], axis=0
        )
        reals, imags = [], []
        for inner in range(width):
            freq = block * width + inner
            field = jnp.concatenate([third[freq], third[NGRID + freq]], axis=0)
            moved = jnp.dot(table, field, preferred_element_type=jnp.float32).astype(jnp.bfloat16)
            reals.append(moved[:wide_two])
            imags.append(moved[wide_two:])
        listed = listed_points(block)
        listed = jnp.transpose(jnp.broadcast_to(listed, (8, count)))[:, :1]
        spot = (listed & (width - 1)) * wide_two + ((listed >> 7) & (wide_two - 1))
        chosen = jnp.where(
            lax.broadcasted_iota(jnp.int32, (count, width * wide_two), 1) == spot, 1.0, 0.0
        ).astype(jnp.bfloat16)
        wave = jnp.where(
            lax.broadcasted_iota(jnp.int32, (count, NGRID), 1) == (listed >> 14), 1.0, 0.0
        ).astype(jnp.bfloat16)

        def choose(mask, field):
            return jnp.dot(mask, field, preferred_element_type=jnp.float32)

        re = choose(chosen, jnp.concatenate(reals, axis=0))
        im = choose(chosen, jnp.concatenate(imags, axis=0))
        both = choose(wave, spread[...])
        cosine, sine = both[:, :lanes], both[:, lanes:]
        z_re = (cosine * re + sine * im).astype(jnp.bfloat16)
        z_im = (cosine * im - sine * re).astype(jnp.bfloat16)
        parts = []
        for low in range(0, BLOCK_ROWS, half):
            for z in (z_re, z_im):
                starts = range(low, count, BLOCK_ROWS)
                parts.append(jnp.concatenate([z[at : at + half] for at in starts], axis=0))
        return jnp.dot(
            jnp.concatenate(parts, axis=1), pack[...], preferred_element_type=jnp.float32
        )

    def sum_copy(distance):
        other, at = block_place(distance)
        return pltpu.make_async_remote_copy(
            src_ref=sums.at[distance], dst_ref=inbox.at[distance],
            send_sem=sum_send.at[distance], recv_sem=sum_recv.at[distance],
            device_id=at, device_id_type=MESH,
        )

    pl.semaphore_wait(barrier, greeted)

    @pl.loop(1, blocks, unroll=5)
    def _(distance):
        sums[distance] = partial_sums(lax.rem(me + distance, blocks)).astype(jnp.bfloat16)
        sum_copy(distance).start()

    total = partial_sums(me)
    for distance in range(1, blocks):
        sum_copy(distance).wait_recv()
        total = total + inbox[distance].astype(jnp.float32)
    elements = total.astype(jnp.bfloat16).astype(jnp.float32)
    weighted = (elements * weight).astype(jnp.bfloat16)
    cols = [elements[(one + 1) * half - col_count : (one + 1) * half] for one in range(n_pair)]
    cols = jnp.concatenate(cols, axis=0).astype(jnp.bfloat16)
    col_out[...] = cols
    for one in range(n_pair):
        row_out[one] = weighted[one * half : (one + 1) * half]
    row_slot = pair_at * n_gcol + gcol_at
    col_slot = pair_at * n_grow + grow_at
    row_copies, col_copies = [], []
    for far in range(n_pair):
        other = lax.rem(pair_at + far, n_pair)
        behind = lax.rem(pair_at + n_pair - far, n_pair)
        for step in range(n_grow):
            if far or step:
                number = far * n_grow + step
                copy = pltpu.make_async_remote_copy(
                    src_ref=col_out, dst_ref=col_in.at[col_slot],
                    send_sem=col_send.at[number], recv_sem=col_recv.at[col_slot],
                    device_id=place(other, lax.rem(grow_at + step, n_grow), gcol_at),
                    device_id_type=MESH,
                )
                copy.start()
                source = behind * n_grow + lax.rem(grow_at + n_grow - step, n_grow)
                col_copies.append((copy, source))
        for step in range(n_gcol):
            if far or step:
                number = far * n_gcol + step
                copy = pltpu.make_async_remote_copy(
                    src_ref=row_out.at[other], dst_ref=row_in.at[row_slot],
                    send_sem=row_send.at[number], recv_sem=row_recv.at[row_slot],
                    device_id=place(other, grow_at, lax.rem(gcol_at + step, n_gcol)),
                    device_id_type=MESH,
                )
                copy.start()
                source = behind * n_gcol + lax.rem(gcol_at + n_gcol - step, n_gcol)
                row_copies.append((copy, source))
    col_in[col_slot] = cols
    row_in[row_slot] = row_out[pair_at]
    for _, source in col_copies:
        arrival(col_out, col_in.at[source], col_send.at[0], col_recv.at[source]).wait_recv()
    lane = lax.broadcasted_iota(jnp.int32, (out.shape[2], 4 * pairs), 1)
    tables = {}
    for one in range(n_pair):
        pieces = []
        for target in range(n_pair):
            for grow in range(n_grow):
                piece = col_in[one * n_grow + grow].astype(jnp.float32)
                pieces.append(piece[target * col_count : (target + 1) * col_count])
        straight = jnp.where(lane >= 2 * pairs, jnp.concatenate(pieces, axis=0), 0.0)
        crossed = jnp.where(
            lane >= 3 * pairs,
            pltpu.roll(straight, pairs, 1),
            jnp.where(lane >= 2 * pairs, -pltpu.roll(straight, 3 * pairs, 1), 0.0),
        )
        for part, table in enumerate((straight, crossed)):
            tables[one, 1, part] = table.astype(jnp.bfloat16)
            tables[one, 0, part] = pltpu.roll(table, 2 * pairs, 1).astype(jnp.bfloat16)
    for _, source in row_copies:
        arrival(row_out.at[0], row_in.at[source], row_send.at[0], row_recv.at[source]).wait_recv()
    rows = [
        jnp.concatenate([row_in[one * n_gcol + gcol] for gcol in range(n_gcol)], axis=0)
        for one in range(n_pair)
    ]
    rows = jnp.concatenate(rows, axis=1)
    for low in range(2):
        for part in range(2):
            table = jnp.concatenate([tables[one, low, part] for one in range(n_pair)], axis=1)
            made = lax.dot_general(
                rows, table, (((1,), (1,)), ((), ())), preferred_element_type=jnp.float32
            )
            kept = min(half, row_count - low * half)
            for gcol in range(n_gcol):
                start = gcol * row_count + low * half
                out[part, start : start + kept, :] = made[gcol * half : gcol * half + kept]
    for distance in range(1, blocks):
        sum_copy(distance).wait_send()
    for copy, _ in col_copies + row_copies:
        copy.wait_send()


def fixed_table():
    freq = np.arange(NGRID, dtype=np.int32)
    angle = (freq[:, None] * freq[None, :] % NGRID).astype(np.float32) * np.float32(2.0 * math.pi / NGRID)
    scale = np.float32(1.0 / math.sqrt(NGRID))
    cosine = np.cos(angle) * scale
    sine = np.sin(angle) * scale
    return np.block([[cosine, sine], [-sine, cosine]]).astype(jnp.bfloat16)


def on_device(valence, conduction, pair_bands, e_val, e_cond, g_index, slab_index):
    n_pair = lax.axis_size("pair")
    n_grow = lax.axis_size("grow")
    n_gcol = lax.axis_size("gcol")
    blocks = n_grow * n_gcol
    _, bands_all, planes, merged = valence.shape
    pairs = pair_bands.size
    row_count = g_index.size // (n_pair * blocks)
    col_count = slab_index.size // (n_pair * blocks)
    if (planes, pairs, n_pair, pair_bands.shape[0], row_count + col_count) != (8, 32, 2, 1, BLOCK_ROWS):
        return on_device_general(valence, conduction, pair_bands, e_val, e_cond, g_index, slab_index)
    lanes = pairs * planes
    half = BLOCK_ROWS // 2
    width = 4 * pairs
    vmem = pl.BlockSpec(memory_space=pltpu.VMEM)
    smem = pl.BlockSpec(memory_space=pltpu.SMEM)
    hbm = pl.BlockSpec(memory_space=pltpu.HBM)
    sem = pltpu.SemaphoreType.DMA
    bf16 = jnp.bfloat16
    return pl.pallas_call(
        functools.partial(slab_kernel, (n_pair, n_grow, n_gcol), row_count),
        out_shape=jax.ShapeDtypeStruct(
            (2, n_gcol * row_count, n_pair * n_grow * col_count), jnp.float32
        ),
        in_specs=[hbm, hbm, smem, hbm, hbm, hbm, hbm, hbm],
        out_specs=vmem,
        scratch_shapes=[
            pltpu.SMEM(pair_bands.shape, jnp.int32),
            pltpu.SMEM(e_val.shape, jnp.float32),
            pltpu.VMEM(conduction.shape, bf16),
            pltpu.VMEM((g_index.size // 128, 128), jnp.int32),
            pltpu.VMEM((slab_index.size // 128, 128), jnp.int32),
            pltpu.VMEM((2 * NGRID, 2 * NGRID), bf16),
            *[pltpu.VMEM((2, bands_all, planes, CHUNK * NGRID), bf16)] * SLOTS,
            *[pltpu.VMEM((lanes // 128, 2 * NGRID * PITCH, 128), jnp.float32)] * 2,
            pltpu.VMEM((2 * NGRID, NGRID, lanes), bf16),
            pltpu.VMEM((4 * lanes, width), bf16),
            pltpu.VMEM((NGRID, 2 * lanes), bf16),
            pltpu.VMEM((blocks, BLOCK_ROWS, width), bf16),
            pltpu.VMEM((blocks, BLOCK_ROWS, width), bf16),
            pltpu.VMEM((n_pair, half, width), bf16),
            pltpu.VMEM((n_pair * n_gcol, half, width), bf16),
            pltpu.VMEM((n_pair * col_count, width), bf16),
            pltpu.VMEM((n_pair * n_grow, n_pair * col_count, width), bf16),
            sem((SLOTS,)),
            sem((6,)),
            sem((blocks,)), sem((blocks,)),
            sem((n_pair * n_gcol,)), sem((n_pair * n_gcol,)),
            sem((n_pair * n_grow,)), sem((n_pair * n_grow,)),
        ],
        compiler_params=pltpu.CompilerParams(
            collective_id=0, has_side_effects=True, vmem_limit_bytes=56 * 2**20
        ),
        name="slab",
    )(
        pair_bands, e_val, e_cond, valence, conduction,
        g_index.reshape(-1, 128), slab_index.reshape(-1, 128), jnp.asarray(fixed_table()),
    )


def solution(mesh):
    in_specs = (
        P(None, None, ("grow", "gcol"), None),
        P(None, "pair", ("grow", "gcol"), None),
        P("pair", None),
        P(),
        P("pair"),
        P(),
        P(),
    )
    out_specs = P(None, ("pair", "grow"), "gcol")
    return jax.shard_map(
        on_device, mesh=mesh, in_specs=in_specs, out_specs=out_specs, check_vma=False
    )
```

```python
import functools
import math

import jax
import jax.numpy as jnp
import numpy as np
from jax import lax
from jax.experimental import pallas as pl
from jax.experimental.pallas import tpu as pltpu
from jax.sharding import PartitionSpec as P

NGRID = 128


def transform_table(count, positions):
    freq = jnp.arange(count, dtype=jnp.int32)
    phase = freq[:, None] * positions[None, :] % count
    angle = phase.astype(jnp.float32) * (2.0 * math.pi / count)
    scale = 1.0 / math.sqrt(count)
    cosine = (jnp.cos(angle) * scale).astype(jnp.bfloat16)
    sine = (jnp.sin(angle) * scale).astype(jnp.bfloat16)
    upper = jnp.stack([cosine, sine], axis=1)
    lower = jnp.stack([-sine, cosine], axis=1)
    return jnp.stack([upper, lower])


def on_device_general(valence, conduction, pair_bands, e_val, e_cond, g_index, slab_index):
    n_pair = lax.axis_size("pair")
    n_grow = lax.axis_size("grow")
    n_gcol = lax.axis_size("gcol")
    grow_at = lax.axis_index("grow")
    gcol_at = lax.axis_index("gcol")
    planes = valence.shape[2]
    bands_here, partners = pair_bands.shape
    pairs_here = bands_here * partners
    total_pairs = pairs_here * n_pair
    picked = jnp.take(valence, pair_bands.reshape(-1), axis=1).astype(jnp.float32)
    cond_rep = jnp.repeat(conduction, partners, axis=1).astype(jnp.float32)
    real_part = picked[0] * cond_rep[0] + picked[1] * cond_rep[1]
    imag_part = picked[0] * cond_rep[1] - picked[1] * cond_rep[0]
    density = jnp.stack([real_part, imag_part]).astype(jnp.bfloat16)
    density = jnp.transpose(density.reshape(2, pairs_here, planes, NGRID, NGRID), (0, 2, 3, 4, 1))
    natural = transform_table(NGRID, jnp.arange(NGRID, dtype=jnp.int32))
    third = jnp.einsum(
        "okix,iabxp->oabkp", natural, density, preferred_element_type=jnp.float32
    ).astype(jnp.bfloat16)
    second = jnp.einsum(
        "okix,iaxbp->oakbp", natural, third, preferred_element_type=jnp.float32
    ).astype(jnp.bfloat16)
    moved = lax.all_to_all(second, ("grow", "gcol"), split_axis=3, concat_axis=1, tiled=True)
    positions = jnp.arange(NGRID, dtype=jnp.int32)
    wide_two = NGRID
    base_three = (grow_at * n_gcol + gcol_at) * planes
    table_first = transform_table(NGRID, positions)
    elements = jnp.einsum(
        "okix,ixabp->okabp", table_first, moved, preferred_element_type=jnp.float32
    ).astype(jnp.bfloat16)
    flat = elements.reshape(2, -1, pairs_here)

    def local_offset(index):
        first_q = index // (NGRID * NGRID)
        second_q = index // NGRID % NGRID
        third_q = index % NGRID
        return (first_q * wide_two + second_q) * planes + third_q - base_three

    row_count = g_index.shape[0] // (n_pair * n_grow * n_gcol)
    row_ids = g_index.reshape(n_pair, n_grow, n_gcol, row_count)[:, grow_at, gcol_at]
    rows = jnp.take(flat, local_offset(row_ids).reshape(-1), axis=1).reshape(
        2, n_pair, row_count, pairs_here
    )
    gaps = jnp.take(e_val, pair_bands) - e_cond[:, None]
    weight = (2.0 / (gaps * math.sqrt(total_pairs))).reshape(-1)
    weighted = (rows.astype(jnp.float32) * weight).astype(jnp.bfloat16)
    col_count = slab_index.shape[0] // (n_pair * n_grow * n_gcol)
    col_ids = slab_index.reshape(n_gcol, n_pair, n_grow, col_count)[gcol_at, :, grow_at]
    cols = jnp.take(flat, local_offset(col_ids).reshape(-1), axis=1).reshape(
        2, n_pair, col_count, pairs_here
    )
    row_block = lax.all_to_all(weighted, "pair", split_axis=1, concat_axis=3, tiled=True).reshape(
        2, row_count, total_pairs
    )
    spread = lax.all_gather(
        cols.reshape(2, n_pair, 1, col_count, pairs_here), "grow", axis=2, tiled=True
    )
    slab = lax.all_gather(spread, "pair", axis=4, tiled=True).reshape(2, -1, total_pairs)
    conjugate = jnp.stack([jnp.stack([slab[0], slab[1]]), jnp.stack([-slab[1], slab[0]])])
    return jnp.einsum(
        "irk,oick->orc",
        lax.all_gather(row_block, "gcol", axis=1, tiled=True),
        conjugate,
        preferred_element_type=jnp.float32,
    )


CHUNK = 16
PITCH = 17
SLOTS = 3
BLOCK_ROWS = 128
MESH = pl.DeviceIdType.MESH


def slab_kernel(
    sizes, row_count, bands_in, e_val_in, e_cond, val, cond_in, g_rows_in, slab_rows_in, t3_in, out,
    bands, e_val, cond, g_rows, slab_rows, t3,
    slot_a, slot_b, slot_c, stage_a, stage_b, third, pack, spread, sums, inbox, row_out, row_in, col_out, col_in,
    sems, load_sems, sum_send, sum_recv, row_send, row_recv, col_send, col_recv,
):
    n_pair, n_grow, n_gcol = sizes
    blocks = n_grow * n_gcol
    pair_at = lax.axis_index("pair")
    grow_at = lax.axis_index("grow")
    gcol_at = lax.axis_index("gcol")
    me = grow_at * n_gcol + gcol_at
    half = BLOCK_ROWS // 2
    col_count = BLOCK_ROWS - row_count
    pairs = bands.shape[1]
    stages = (stage_a, stage_b)
    held = (slot_a, slot_b, slot_c)
    slots = len(held)
    planes, wide = slot_a.shape[2], slot_a.shape[3]
    lanes = pairs * planes
    chunks = NGRID // CHUNK

    def place(pair, grow, gcol):
        return {"pair": pair, "grow": grow, "gcol": gcol}

    def arrival(src, dst, send, recv):
        at = place(lax.rem(pair_at + 1, n_pair), grow_at, gcol_at)
        return pltpu.make_async_remote_copy(
            src_ref=src, dst_ref=dst, send_sem=send, recv_sem=recv, device_id=at, device_id_type=MESH
        )

    def block_place(distance):
        other = lax.rem(me + distance, blocks)
        return other, place(pair_at, other // n_gcol, lax.rem(other, n_gcol))

    def fetch(chunk):
        return pltpu.make_async_copy(
            val.at[:, :, :, pl.ds(chunk * wide, wide)], held[chunk % slots], sems.at[chunk % slots]
        )

    loads = [
        pltpu.make_async_copy(src, dst, load_sems.at[number])
        for number, (src, dst) in enumerate(
            ((bands_in, bands), (e_val_in, e_val), (t3_in, t3), (cond_in, cond), (g_rows_in, g_rows), (slab_rows_in, slab_rows))
        )
    ]
    for load in loads:
        load.start()
    for chunk in range(slots - 1):
        fetch(chunk).start()

    barrier = pltpu.get_barrier_semaphore()
    greeted = 0
    for distance in range(1, blocks):
        pl.semaphore_signal(barrier, inc=1, device_id=block_place(distance)[1], device_id_type=MESH)
        greeted += 1
    for far in range(1, n_pair):
        other = lax.rem(pair_at + far, n_pair)
        for step in range(n_gcol):
            at = place(other, grow_at, lax.rem(gcol_at + step, n_gcol))
            pl.semaphore_signal(barrier, inc=1, device_id=at, device_id_type=MESH)
            greeted += 1
        for step in range(1, n_grow):
            at = place(other, lax.rem(grow_at + step, n_grow), gcol_at)
            pl.semaphore_signal(barrier, inc=1, device_id=at, device_id_type=MESH)
            greeted += 1

    for load in loads:
        load.wait()
    source = lax.broadcasted_iota(jnp.int32, pack.shape, 0)
    target = source // lanes * pairs + source % lanes // planes
    pack[...] = jnp.where(
        target == lax.broadcasted_iota(jnp.int32, pack.shape, 1), 1.0, 0.0
    ).astype(jnp.bfloat16)
    plane = lax.broadcasted_iota(jnp.int32, (NGRID, lanes), 1) % planes + me * planes
    expand = jnp.where(
        lax.broadcasted_iota(jnp.int32, (NGRID, lanes), 0) == plane, 1.0, 0.0
    ).astype(jnp.bfloat16)
    for part in range(2):
        spread[:, part * lanes : (part + 1) * lanes] = jnp.dot(
            t3[:NGRID, part * NGRID : (part + 1) * NGRID], expand, preferred_element_type=jnp.float32
        ).astype(jnp.bfloat16)
    spot_of = lax.broadcasted_iota(jnp.int32, (1, 4 * pairs), 1) % pairs
    energy = jnp.zeros((1, 4 * pairs), jnp.float32)
    for pair in range(pairs):
        energy = jnp.where(spot_of == pair, e_val[bands[0, pair]], energy)
    weight = 2.0 / ((energy - e_cond[0]) * math.sqrt(pairs * n_pair))

    groups = 2 * NGRID // 8 // CHUNK

    def settle(chunk, group):
        for inner in range(8):
            start = pl.multiple_of(group * (8 * PITCH), 8) + inner * PITCH
            for part in range(lanes // 128):
                third[group * 8 + inner, chunk * CHUNK : (chunk + 1) * CHUNK, part * 128 : (part + 1) * 128] = (
                    stages[chunk % 2][part, pl.ds(start, CHUNK), :].astype(jnp.bfloat16)
                )

    for chunk in range(chunks):
        slot = held[chunk % slots]
        fetch(chunk).wait()
        if chunk + slots - 1 < chunks:
            fetch(chunk + slots - 1).start()

        @pl.loop(0, CHUNK, unroll=8)
        def _(step):
            there = pl.ds(pl.multiple_of(chunk * wide + step * NGRID, NGRID), NGRID)
            here = pl.ds(pl.multiple_of(step * NGRID, NGRID), NGRID)
            c_re = cond[0, 0, :, there].astype(jnp.float32)
            c_im = cond[1, 0, :, there].astype(jnp.float32)
            reals, imags = [], []
            for pair in range(pairs):
                v_re = slot[0, bands[0, pair], :, here].astype(jnp.float32)
                v_im = slot[1, bands[0, pair], :, here].astype(jnp.float32)
                reals.append(v_re * c_re + v_im * c_im)
                imags.append(v_re * c_im - v_im * c_re)
            density = jnp.concatenate(
                [jnp.concatenate(reals, axis=0), jnp.concatenate(imags, axis=0)], axis=1
            ).astype(jnp.bfloat16)
            moved = lax.dot_general(
                t3[...], density, (((1,), (1,)), ((), ())), preferred_element_type=jnp.float32
            )
            for part in range(lanes // 128):
                stages[chunk % 2][part, pl.ds(step, 2 * NGRID, stride=PITCH), :] = moved[
                    :, part * 128 : (part + 1) * 128
                ]

            if chunk:
                for group in range(groups):
                    settle(chunk - 1, step * groups + group)

    @pl.loop(0, 2 * NGRID // 8)
    def _(group):
        settle(chunks - 1, group)

    width = NGRID // blocks
    wide_two = NGRID // n_gcol
    count = n_pair * BLOCK_ROWS
    across = lax.broadcasted_iota(jnp.int32, (1, BLOCK_ROWS), 1)

    def listed_points(block):
        grow, gcol = block // n_gcol, lax.rem(block, n_gcol)
        found = []
        for pair in range(n_pair):
            start = ((pair * n_grow + grow) * n_gcol + gcol) * row_count
            line, offset = start // 128, lax.rem(start, 128)
            back = lax.rem(128 - offset, 128)
            split = 128 - offset
            here = pltpu.roll(g_rows[pl.ds(line, 1), :], back, 1)
            after = pltpu.roll(g_rows[pl.ds(lax.rem(line + 1, g_rows.shape[0]), 1), :], back, 1)
            start = ((gcol * n_pair + pair) * n_grow + grow) * col_count
            line, offset = start // 128, lax.rem(start, 128)
            cols = pltpu.roll(
                slab_rows[pl.ds(line, 1), :], lax.rem(row_count + 128 - offset, 128), 1
            )
            rows = jnp.where(across < split, here, after)
            found.append(jnp.where(across < row_count, rows, cols))
        return jnp.concatenate(found, axis=1)

    def partial_sums(block):
        first_row = pl.multiple_of(lax.rem(block, n_gcol) * wide_two, wide_two)
        table = jnp.concatenate(
            [t3[pl.ds(first_row, wide_two), :], t3[pl.ds(first_row + NGRID, wide_two), :]], axis=0
        )
        reals, imags = [], []
        for inner in range(width):
            freq = block * width + inner
            field = jnp.concatenate([third[freq], third[NGRID + freq]], axis=0)
            moved = jnp.dot(table, field, preferred_element_type=jnp.float32).astype(jnp.bfloat16)
            reals.append(moved[:wide_two])
            imags.append(moved[wide_two:])
        listed = listed_points(block)
        listed = jnp.transpose(jnp.broadcast_to(listed, (8, count)))[:, :1]
        spot = (listed & (width - 1)) * wide_two + ((listed >> 7) & (wide_two - 1))
        chosen = jnp.where(
            lax.broadcasted_iota(jnp.int32, (count, width * wide_two), 1) == spot, 1.0, 0.0
        ).astype(jnp.bfloat16)
        wave = jnp.where(
            lax.broadcasted_iota(jnp.int32, (count, NGRID), 1) == (listed >> 14), 1.0, 0.0
        ).astype(jnp.bfloat16)

        def choose(mask, field):
            return jnp.dot(mask, field, preferred_element_type=jnp.float32)

        re = choose(chosen, jnp.concatenate(reals, axis=0))
        im = choose(chosen, jnp.concatenate(imags, axis=0))
        both = choose(wave, spread[...])
        cosine, sine = both[:, :lanes], both[:, lanes:]
        z_re = (cosine * re + sine * im).astype(jnp.bfloat16)
        z_im = (cosine * im - sine * re).astype(jnp.bfloat16)
        parts = []
        for low in range(0, BLOCK_ROWS, half):
            for z in (z_re, z_im):
                starts = range(low, count, BLOCK_ROWS)
                parts.append(jnp.concatenate([z[at : at + half] for at in starts], axis=0))
        return jnp.dot(
            jnp.concatenate(parts, axis=1), pack[...], preferred_element_type=jnp.float32
        )

    def sum_copy(distance):
        other, at = block_place(distance)
        return pltpu.make_async_remote_copy(
            src_ref=sums.at[distance], dst_ref=inbox.at[distance],
            send_sem=sum_send.at[distance], recv_sem=sum_recv.at[distance],
            device_id=at, device_id_type=MESH,
        )

    pl.semaphore_wait(barrier, greeted)

    @pl.loop(1, blocks, unroll=5)
    def _(distance):
        sums[distance] = partial_sums(lax.rem(me + distance, blocks)).astype(jnp.bfloat16)
        sum_copy(distance).start()

    total = partial_sums(me)
    for distance in range(1, blocks):
        sum_copy(distance).wait_recv()
        total = total + inbox[distance].astype(jnp.float32)
    elements = total.astype(jnp.bfloat16).astype(jnp.float32)
    weighted = (elements * weight).astype(jnp.bfloat16)
    cols = [elements[(one + 1) * half - col_count : (one + 1) * half] for one in range(n_pair)]
    cols = jnp.concatenate(cols, axis=0).astype(jnp.bfloat16)
    col_out[...] = cols
    for one in range(n_pair):
        row_out[one] = weighted[one * half : (one + 1) * half]
    row_slot = pair_at * n_gcol + gcol_at
    col_slot = pair_at * n_grow + grow_at
    row_copies, col_copies = [], []
    for far in range(n_pair):
        other = lax.rem(pair_at + far, n_pair)
        behind = lax.rem(pair_at + n_pair - far, n_pair)
        for step in range(n_grow):
            if far or step:
                number = far * n_grow + step
                copy = pltpu.make_async_remote_copy(
                    src_ref=col_out, dst_ref=col_in.at[col_slot],
                    send_sem=col_send.at[number], recv_sem=col_recv.at[col_slot],
                    device_id=place(other, lax.rem(grow_at + step, n_grow), gcol_at),
                    device_id_type=MESH,
                )
                copy.start()
                source = behind * n_grow + lax.rem(grow_at + n_grow - step, n_grow)
                col_copies.append((copy, source))
        for step in range(n_gcol):
            if far or step:
                number = far * n_gcol + step
                copy = pltpu.make_async_remote_copy(
                    src_ref=row_out.at[other], dst_ref=row_in.at[row_slot],
                    send_sem=row_send.at[number], recv_sem=row_recv.at[row_slot],
                    device_id=place(other, grow_at, lax.rem(gcol_at + step, n_gcol)),
                    device_id_type=MESH,
                )
                copy.start()
                source = behind * n_gcol + lax.rem(gcol_at + n_gcol - step, n_gcol)
                row_copies.append((copy, source))
    col_in[col_slot] = cols
    row_in[row_slot] = row_out[pair_at]
    for _, source in col_copies:
        arrival(col_out, col_in.at[source], col_send.at[0], col_recv.at[source]).wait_recv()
    lane = lax.broadcasted_iota(jnp.int32, (out.shape[1], 4 * pairs), 1)
    tables = {}
    for one in range(n_pair):
        pieces = []
        for target in range(n_pair):
            for grow in range(n_grow):
                piece = col_in[one * n_grow + grow].astype(jnp.float32)
                pieces.append(piece[target * col_count : (target + 1) * col_count])
        straight = jnp.where(lane >= 2 * pairs, jnp.concatenate(pieces, axis=0), 0.0)
        crossed = jnp.where(
            lane >= 3 * pairs,
            pltpu.roll(straight, pairs, 1),
            jnp.where(lane >= 2 * pairs, -pltpu.roll(straight, 3 * pairs, 1), 0.0),
        )
        for part, table in enumerate((straight, crossed)):
            tables[one, 1, part] = table.astype(jnp.bfloat16)
            tables[one, 0, part] = pltpu.roll(table, 2 * pairs, 1).astype(jnp.bfloat16)
    for _, source in row_copies:
        arrival(row_out.at[0], row_in.at[source], row_send.at[0], row_recv.at[source]).wait_recv()
    rows = [
        jnp.concatenate([row_in[one * n_gcol + gcol] for gcol in range(n_gcol)], axis=0)
        for one in range(n_pair)
    ]
    rows = jnp.concatenate(rows, axis=1)
    for part in range(2):
        made = []
        for low in range(2):
            table = jnp.concatenate([tables[one, low, part] for one in range(n_pair)], axis=1)
            made.append(
                lax.dot_general(
                    table, rows, (((1,), (1,)), ((), ())), preferred_element_type=jnp.float32
                )
            )
        for gcol in range(n_gcol):
            for low in range(2):
                kept = min(half, row_count - low * half)
                start = gcol * row_count + low * half
                out[part, :, start : start + kept] = made[low][:, gcol * half : gcol * half + kept]
    for distance in range(1, blocks):
        sum_copy(distance).wait_send()
    for copy, _ in col_copies + row_copies:
        copy.wait_send()


def fixed_table():
    freq = np.arange(NGRID, dtype=np.int32)
    angle = (freq[:, None] * freq[None, :] % NGRID).astype(np.float32) * np.float32(2.0 * math.pi / NGRID)
    scale = np.float32(1.0 / math.sqrt(NGRID))
    cosine = np.cos(angle) * scale
    sine = np.sin(angle) * scale
    return np.block([[cosine, sine], [-sine, cosine]]).astype(jnp.bfloat16)


def on_device(valence, conduction, pair_bands, e_val, e_cond, g_index, slab_index):
    n_pair = lax.axis_size("pair")
    n_grow = lax.axis_size("grow")
    n_gcol = lax.axis_size("gcol")
    blocks = n_grow * n_gcol
    _, bands_all, planes, merged = valence.shape
    pairs = pair_bands.size
    row_count = g_index.size // (n_pair * blocks)
    col_count = slab_index.size // (n_pair * blocks)
    if (planes, pairs, n_pair, pair_bands.shape[0], row_count + col_count) != (8, 32, 2, 1, BLOCK_ROWS):
        return on_device_general(valence, conduction, pair_bands, e_val, e_cond, g_index, slab_index)
    lanes = pairs * planes
    half = BLOCK_ROWS // 2
    width = 4 * pairs
    vmem = pl.BlockSpec(memory_space=pltpu.VMEM)
    smem = pl.BlockSpec(memory_space=pltpu.SMEM)
    hbm = pl.BlockSpec(memory_space=pltpu.HBM)
    sem = pltpu.SemaphoreType.DMA
    bf16 = jnp.bfloat16
    made = pl.pallas_call(
        functools.partial(slab_kernel, (n_pair, n_grow, n_gcol), row_count),
        out_shape=jax.ShapeDtypeStruct(
            (2, n_pair * n_grow * col_count, n_gcol * row_count), jnp.float32
        ),
        in_specs=[hbm, hbm, smem, hbm, hbm, hbm, hbm, hbm],
        out_specs=vmem,
        scratch_shapes=[
            pltpu.SMEM(pair_bands.shape, jnp.int32),
            pltpu.SMEM(e_val.shape, jnp.float32),
            pltpu.VMEM(conduction.shape, bf16),
            pltpu.VMEM((g_index.size // 128, 128), jnp.int32),
            pltpu.VMEM((slab_index.size // 128, 128), jnp.int32),
            pltpu.VMEM((2 * NGRID, 2 * NGRID), bf16),
            *[pltpu.VMEM((2, bands_all, planes, CHUNK * NGRID), bf16)] * SLOTS,
            *[pltpu.VMEM((lanes // 128, 2 * NGRID * PITCH, 128), jnp.float32)] * 2,
            pltpu.VMEM((2 * NGRID, NGRID, lanes), bf16),
            pltpu.VMEM((4 * lanes, width), bf16),
            pltpu.VMEM((NGRID, 2 * lanes), bf16),
            pltpu.VMEM((blocks, BLOCK_ROWS, width), bf16),
            pltpu.VMEM((blocks, BLOCK_ROWS, width), bf16),
            pltpu.VMEM((n_pair, half, width), bf16),
            pltpu.VMEM((n_pair * n_gcol, half, width), bf16),
            pltpu.VMEM((n_pair * col_count, width), bf16),
            pltpu.VMEM((n_pair * n_grow, n_pair * col_count, width), bf16),
            sem((SLOTS,)),
            sem((6,)),
            sem((blocks,)), sem((blocks,)),
            sem((n_pair * n_gcol,)), sem((n_pair * n_gcol,)),
            sem((n_pair * n_grow,)), sem((n_pair * n_grow,)),
        ],
        compiler_params=pltpu.CompilerParams(
            collective_id=0, has_side_effects=True, vmem_limit_bytes=56 * 2**20
        ),
        name="slab",
    )(
        pair_bands, e_val, e_cond, valence, conduction,
        g_index.reshape(-1, 128), slab_index.reshape(-1, 128), jnp.asarray(fixed_table()),
    )
    return jnp.transpose(made, (0, 2, 1))


def solution(mesh):
    in_specs = (
        P(None, None, ("grow", "gcol"), None),
        P(None, "pair", ("grow", "gcol"), None),
        P("pair", None),
        P(),
        P("pair"),
        P(),
        P(),
    )
    out_specs = P(None, ("pair", "grow"), "gcol")
    return jax.shard_map(
        on_device, mesh=mesh, in_specs=in_specs, out_specs=out_specs, check_vma=False
    )
```
